512 devices in a mesh: section: 32 (over x, y), expert: 4 (over z_hi), dp: 4 (over z_lo, core).
Axes of the slice: x: 4, y: 8, z: 8 (z_hi: 4, z_lo: 2; z = z_hi * 2 + z_lo), core: 2. Of those that a mesh axis runs over, the one named last changes fastest.
Arguments:
- state_in: bfloat16 [2, 32, 256, 3584], P(None, 'section', 'dp', 'expert'), may hold values from -1.5 to 1.5
- saved_inputs: bfloat16 [4, 2, 32, 256, 3584], P(None, None, 'section', 'dp', 'expert'), may hold values from -6 to 6
- slot_rows: int32 [4, 2, 32, 256], P(None, None, 'section', 'dp'), may hold values from 0 to 63, as said below
- combine: float32 [4, 2, 32, 256], P(None, None, 'section', 'dp'), may hold values from 0.4 to 0.7
- w_gate: bfloat16 [32, 3584, 1024], P('section', 'expert', 'dp'), may hold values from -0.09375 to 0.09375
- w_up: bfloat16 [32, 3584, 1024], P('section', 'expert', 'dp'), may hold values from -0.125 to 0.125
- w_down: bfloat16 [32, 1024, 3584], P('section', 'dp', 'expert'), may hold values from -0.25 to 0.25
Outputs:
- state_out: bfloat16 [2, 32, 256, 3584], P(None, 'section', 'dp', 'expert')
- grad_gate: bfloat16 [32, 3584, 1024], P('section', 'expert', 'dp')
- grad_up: bfloat16 [32, 3584, 1024], P('section', 'expert', 'dp')
The draws below stay inside these ranges and needn't reach their ends.
Inputs may be any that keep to these rules, and one draw needn't show every extreme that they name: `slot_rows`: each aligned block of 64 slots holds every one of the 64 token rows of the block's group once, counted from the group's first token.
All inputs are finite; a program needn't handle non-finite values.
Results may differ from the reference program's by a relative error of at most 0.035.
Values may be sent and summed in bfloat16 or wider, within the bound.
A program may use at most 64 MiB of HBM per device.

```python
import jax
import jax.numpy as jnp
from jax import lax

D = 3584
HID = 1024
STEPS = 4
TOK_DP = 64
SLOT_DP = 64
TOKENS = 256
SLOTS = 256
N_SECTION = 32
N_EXPERT = 4
N_DP = 4


def draw_slot_rows(key, part):
    key = jax.random.fold_in(key, 11)
    scores = jax.random.randint(key, (STEPS, 2, N_SECTION, N_DP, TOK_DP), 0, 1 << 16)
    scores = scores * TOK_DP + jnp.arange(TOK_DP, dtype=jnp.int32)
    ranking = jnp.argsort(scores, axis=-1, stable=True)
    chosen = ranking[..., :SLOT_DP]
    return chosen.reshape(STEPS, 2, N_SECTION, SLOTS).astype(jnp.int32)


def block_levels(key, shape, split, smallest, largest):
    level, own = 1.0, jax.random.fold_in(key, 6)
    for position, shards_of in split:
        heights = jnp.exp(jax.random.uniform(jax.random.fold_in(own, position), (shards_of,), jnp.float32, smallest / len(split), largest / len(split)))
        level = level * jnp.repeat(heights, shape[position] // shards_of).reshape([-1 if axis == position else 1 for axis in range(len(shape))])
    return level


def gaussian(rng, dims, spread, bound, split=(), kind=jnp.bfloat16):
    values = spread * jax.random.normal(rng, dims, jnp.float32)
    if split:
        values = values * block_levels(rng, dims, split, -0.22, 0.18)
    return jnp.clip(values, -bound, bound).astype(kind)


def setup_inputs(seed: int = 0) -> dict:
    splits = jax.random.split(jax.random.key(seed), 8)
    return {
        "state_in": gaussian(splits[0], (2, N_SECTION, TOKENS, D), 0.25, 1.5, ((1, 32), (2, 4), (3, 4))),
        "saved_inputs": gaussian(splits[1], (STEPS, 2, N_SECTION, SLOTS, D), 1.0, 6.0, ((2, 32), (3, 4), (4, 4))),
        "slot_rows": draw_slot_rows(jax.random.fold_in(splits[7], 71), 0),
        "combine": jnp.clip(0.4 + 0.29999998 * jax.random.uniform(splits[3], (STEPS, 2, N_SECTION, SLOTS), jnp.float32) ** block_levels(splits[3], (STEPS, 2, N_SECTION, SLOTS), ((2, 32), (3, 4)), -0.2, 0.2), 0.4, 0.7),
        "w_gate": gaussian(splits[4], (N_SECTION, D, HID), D ** -0.5, 0.09375, ((0, 32), (1, 4), (2, 4))),
        "w_up": gaussian(splits[5], (N_SECTION, D, HID), (D // 2) ** -0.5, 0.125, ((0, 32), (1, 4), (2, 4))),
        "w_down": gaussian(splits[6], (N_SECTION, HID, D), (HID // 2) ** -0.5, 0.25, ((0, 32), (1, 4), (2, 4))),
    }


def rounded_sum(partials):
    narrow = lax.optimization_barrier(partials.astype(jnp.bfloat16))
    return jnp.sum(narrow.astype(jnp.float32), axis=0)


def section_layer(operands):
    grads_state, inputs, slot_index, weights, gate_w, up_w, down_w = operands
    col_width = D // N_EXPERT
    hid_share = HID // N_DP
    group_offset = (jnp.arange(SLOTS, dtype=jnp.int32) // SLOT_DP) * TOK_DP
    token_index = slot_index.astype(jnp.int32) + group_offset
    picked = grads_state[token_index]
    slot_grads = (weights[:, None] * picked.astype(jnp.float32)).astype(jnp.bfloat16)
    inputs_q = inputs.astype(jnp.float32).reshape(SLOTS, N_EXPERT, col_width)
    grads_q = slot_grads.astype(jnp.float32).reshape(SLOTS, N_EXPERT, col_width)
    gate_q = gate_w.astype(jnp.float32).reshape(N_EXPERT, col_width, HID)
    up_q = up_w.astype(jnp.float32).reshape(N_EXPERT, col_width, HID)
    down_q = down_w.astype(jnp.float32).reshape(HID, N_EXPERT, col_width)
    pre_gate = rounded_sum(jnp.einsum("sqd,qdh->qsh", inputs_q, gate_q))
    pre_up = rounded_sum(jnp.einsum("sqd,qdh->qsh", inputs_q, up_q))
    hidden_grad = rounded_sum(jnp.einsum("sqd,hqd->qsh", grads_q, down_q))
    sigmoid_gate = jax.nn.sigmoid(pre_gate)
    gate_grad = (hidden_grad * pre_up * sigmoid_gate * (1.0 + pre_gate * (1.0 - sigmoid_gate))).astype(jnp.bfloat16)
    up_grad = (hidden_grad * pre_gate * sigmoid_gate).astype(jnp.bfloat16)
    gate_h = gate_grad.astype(jnp.float32).reshape(SLOTS, N_DP, hid_share)
    up_h = up_grad.astype(jnp.float32).reshape(SLOTS, N_DP, hid_share)
    gate_wh = gate_w.astype(jnp.float32).reshape(D, N_DP, hid_share)
    up_wh = up_w.astype(jnp.float32).reshape(D, N_DP, hid_share)
    partial_terms = jnp.einsum("sph,dph->psd", gate_h, gate_wh) + jnp.einsum("sph,dph->psd", up_h, up_wh)
    added_grad = rounded_sum(partial_terms)
    updated = (picked.astype(jnp.float32) + added_grad).astype(jnp.bfloat16)
    return grads_state.at[token_index].set(updated), gate_grad, up_grad


def section_weight_grads(operands):
    inputs, gate_grad, up_grad = operands
    inputs_g = inputs.astype(jnp.float32).reshape(STEPS, 2, N_DP, SLOT_DP, D)
    gate_g = gate_grad.astype(jnp.float32).reshape(STEPS, 2, N_DP, SLOT_DP, HID)
    up_g = up_grad.astype(jnp.float32).reshape(STEPS, 2, N_DP, SLOT_DP, HID)
    grad_gate = rounded_sum(jnp.einsum("tcgsd,tcgsh->gdh", inputs_g, gate_g)).astype(jnp.bfloat16)
    grad_up = rounded_sum(jnp.einsum("tcgsd,tcgsh->gdh", inputs_g, up_g)).astype(jnp.bfloat16)
    return grad_gate, grad_up


def reference(state_in, saved_inputs, slot_rows, combine, w_gate, w_up, w_down):
    states = [state_in[0], state_in[1]]
    gate_steps = []
    up_steps = []
    for step_index in range(STEPS):
        gate_dirs = []
        up_dirs = []
        for direction in range(2):
            fresh, gate_grad, up_grad = lax.map(section_layer, (states[direction], saved_inputs[step_index, direction], slot_rows[step_index, direction], combine[step_index, direction], w_gate, w_up, w_down))
            states[direction] = fresh
            gate_dirs.append(gate_grad)
            up_dirs.append(up_grad)
        gate_steps.append(jnp.stack(gate_dirs))
        up_steps.append(jnp.stack(up_dirs))
        if step_index + 1 < STEPS:
            states[0] = jnp.roll(states[0], -1, axis=0)
            states[1] = jnp.roll(states[1], 1, axis=0)
    gate_all = jnp.moveaxis(jnp.stack(gate_steps), 2, 0)
    up_all = jnp.moveaxis(jnp.stack(up_steps), 2, 0)
    inputs_all = jnp.moveaxis(saved_inputs, 2, 0)
    grad_gate, grad_up = lax.map(section_weight_grads, (inputs_all, gate_all, up_all))
    return jnp.stack(states), grad_gate, grad_up
```

```python
import jax
import jax.numpy as jnp
from jax import lax
from jax.experimental import pallas as pl
from jax.experimental.pallas import tpu as pltpu
from jax.sharding import PartitionSpec as P

MESH = pl.DeviceIdType.MESH
F32 = jnp.float32
BF16 = jnp.bfloat16


def dot_nn(a, b):
    return lax.dot_general(a, b, (((1,), (0,)), ((), ())), preferred_element_type=F32)


def dot_nt(a, b):
    return lax.dot_general(a, b, (((1,), (1,)), ((), ())), preferred_element_type=F32)


def dot_tn(a, b):
    return lax.dot_general(a, b, (((0,), (0,)), ((), ())), preferred_element_type=F32)


def relay_kernel(
    state_ref, x_ref, rows_ref, comb_ref, wg_ref, wu_ref, wd_ref,
    state_out, gg_out, gu_out,
    xs, wga, wua, wda, st, sn, ppart, precv, ab, hpart, hrecv, act,
    gsend, grecv, psend, gprecv, keep,
    loc_sem, ws_send, ws_recv, wp_send, wp_recv, wf_send, wf_recv,
    pre_s, pre_r, hid_s, hid_r, act_s, act_r, st_s, st_r,
    gs_s, gs_r, gp_s, gp_r,
):
    s = lax.axis_index("section")
    e = lax.axis_index("expert")
    p = lax.axis_index("dp")
    sections = lax.axis_size("section")
    steps = st.shape[0]
    tokens = st.shape[2]
    sib = p + 1 - 2 * lax.rem(p, 2)
    pair = lax.rem(p + 2, 4)
    diag = lax.rem(sib + 2, 4)
    sib_dev = (s, e, sib)
    pair_dev = (s, e, pair)
    below = (lax.rem(s + sections - 1, sections), e, p)
    above = (lax.rem(s + 1, sections), e, p)

    def peer(k):
        return lax.rem(e + k, 4)

    def peer_dev(k):
        return (s, peer(k), p)

    def remote(src, dst, send, recv, dev):
        return pltpu.make_async_remote_copy(
            src_ref=src, dst_ref=dst, send_sem=send, recv_sem=recv,
            device_id=dev, device_id_type=MESH,
        )

    barrier = pltpu.get_barrier_semaphore()
    for dev in (peer_dev(1), peer_dev(2), peer_dev(3), sib_dev, pair_dev, below, above):
        pl.semaphore_signal(barrier, inc=1, device_id=dev, device_id_type=MESH)
    pl.semaphore_wait(barrier, 7)

    weights = ((wg_ref, wga), (wu_ref, wua), (wd_ref, wda))

    def own_to_pair(n):
        src, dst = weights[n]
        return remote(src, dst.at[p], wp_send.at[n], wp_recv.at[n], pair_dev)

    def own_to_sib(n):
        src, dst = weights[n]
        return remote(src, dst.at[p], ws_send.at[n], ws_recv.at[n], sib_dev)

    def pair_to_sib(n):
        dst = weights[n][1]
        return remote(dst.at[pair], dst.at[pair], wf_send.at[n], wf_recv.at[n], sib_dev)

    def local(n):
        src, dst = weights[n]
        return pltpu.make_async_copy(src, dst.at[p], loc_sem.at[n])

    for n in range(3):
        own_to_pair(n).start()
    for n in range(3):
        own_to_sib(n).start()
        local(n).start()

    def chosen(i):
        token = lax.broadcasted_iota(jnp.int32, (tokens, tokens), 0)
        return token == rows_ref[i]

    def sort_rows(i, carry):
        pick = jnp.where(chosen(i), 1.0, 0.0).astype(BF16)
        xs[i] = dot_nn(pick, x_ref[i]).astype(BF16)
        return carry

    lax.fori_loop(0, 2 * steps, sort_rows, 0)
    st[0] = state_ref[...]

    def pre_chunk(t, q):
        x = xs[pl.ds(2 * t, 2)].reshape(2 * tokens, xs.shape[2])
        ppart[t, q, 0] = dot_nn(x, wga[q]).astype(BF16)
        ppart[t, q, 1] = dot_nn(x, wua[q]).astype(BF16)

    def pre_copy(t, k):
        return remote(
            ppart.at[t, peer(k)], precv.at[t, k - 1], pre_s.at[t, k - 1], pre_r.at[t, k - 1], peer_dev(k)
        )

    local(0).wait()
    local(1).wait()
    pre_chunk(0, p)
    own_to_sib(0).wait_recv()
    own_to_sib(1).wait_recv()
    pre_chunk(0, sib)
    own_to_pair(0).wait_recv()
    pair_to_sib(0).start()
    own_to_pair(1).wait_recv()
    pair_to_sib(1).start()
    pre_chunk(0, pair)
    pair_to_sib(0).wait_recv()
    pair_to_sib(1).wait_recv()
    pre_chunk(0, diag)
    for k in (2, 1, 3):
        pre_copy(0, k).start()
    local(2).wait()
    own_to_pair(2).wait_recv()
    pair_to_sib(2).start()
    own_to_sib(2).wait_recv()
    pair_to_sib(2).wait_recv()

    def hid_copy(i, k):
        return remote(hpart.at[i, peer(k)], hrecv.at[i, k - 1], hid_s.at[i, k - 1], hid_r.at[i, k - 1], peer_dev(k))

    def act_copy(i, k):
        return remote(act.at[i, e], act.at[i, e], act_s.at[i, k - 1], act_r.at[i, k - 1], peer_dev(k))

    def act_arrival(i, k):
        there = lax.rem(e + 4 - k, 4)
        return remote(act.at[i, there], act.at[i, there], act_s.at[i, k - 1], act_r.at[i, k - 1], peer_dev(k))

    def st_copy(t, c):
        return remote(sn.at[t, c], st.at[t + 1, c], st_s.at[t, c], st_r.at[t, c], below if c == 0 else above)

    def step(t, carry):
        for c in range(2):
            i = 2 * t + c

            @pl.when(t > 0)
            def _():
                st_copy(t - 1, c).wait_recv()

            weight = jnp.sum(jnp.where(chosen(i), comb_ref[i], 0.0), axis=1, keepdims=True)
            slot_grads = (weight * st[t, c].astype(F32)).astype(BF16)
            for q in range(4):
                hpart[i, q] = dot_nt(slot_grads, wda[q]).astype(BF16)
            for k in (2, 1, 3):
                hid_copy(i, k).start()

        for k in (1, 2, 3):
            pre_copy(t, k).wait_recv()
        pre_gate = ppart[t, e, 0].astype(F32)
        pre_up = ppart[t, e, 1].astype(F32)
        for k in range(3):
            pre_gate += precv[t, k, 0].astype(F32)
            pre_up += precv[t, k, 1].astype(F32)
        sigma = jax.nn.sigmoid(pre_gate)
        ab[0] = pre_up * sigma * (1.0 + pre_gate * (1.0 - sigma))
        ab[1] = pre_gate * sigma

        for c in range(2):
            i = 2 * t + c
            for k in (1, 3, 2):
                hid_copy(i, k).wait_recv()
            hidden = hpart[i, e].astype(F32)
            for k in range(3):
                hidden += hrecv[i, k].astype(F32)
            act[i, e, 0] = (hidden * ab[0, c * tokens:(c + 1) * tokens]).astype(BF16)
            act[i, e, 1] = (hidden * ab[1, c * tokens:(c + 1) * tokens]).astype(BF16)
            for k in (2, 1, 3):
                act_copy(i, k).start()

        @pl.when(t < steps - 1)
        def _():
            def chunk(q, carry):
                pre_chunk(t + 1, q)
                return carry

            lax.fori_loop(0, 4, chunk, 0)
            for k in (2, 1, 3):
                pre_copy(t + 1, k).start()

        for c in range(2):
            i = 2 * t + c
            for k in (1, 3, 2):
                act_arrival(i, k).wait_recv()
            total = st[t, c].astype(F32)
            for q in range(4):
                total += dot_nt(act[i, q, 0], wga[q]) + dot_nt(act[i, q, 1], wua[q])
            sn[t, c] = total.astype(BF16)

            @pl.when(t < steps - 1)
            def _():
                st_copy(t, c).start()

        return carry

    lax.fori_loop(0, steps, step, 0)
    state_out[...] = sn[steps - 1]

    flat = xs[...].reshape(2 * steps * tokens, xs.shape[2])

    def weight_grad(q, n):
        grads = act[:, q, n].reshape(2 * steps * tokens, act.shape[4])
        return dot_tn(flat, grads)

    def sib_copy(m):
        return remote(gsend.at[m], grecv.at[m], gs_s.at[m], gs_r.at[m], sib_dev)

    def pair_copy(n):
        return remote(psend.at[n], gprecv.at[n], gp_s.at[n], gp_r.at[n], pair_dev)

    for n in range(2):
        gsend[n] = weight_grad(diag, n).astype(BF16)
        sib_copy(n).start()
        part = weight_grad(pair, n)
        sib_copy(n).wait_recv()
        psend[n] = (part + grecv[n].astype(F32)).astype(BF16)
        pair_copy(n).start()
    for n in range(2):
        gsend[2 + n] = weight_grad(sib, n).astype(BF16)
        sib_copy(2 + n).start()
    for n in range(2):
        keep[n] = weight_grad(p, n)
    for n in range(2):
        sib_copy(2 + n).wait_recv()
        keep[n] += grecv[2 + n].astype(F32)
    for n, out in ((0, gg_out), (1, gu_out)):
        pair_copy(n).wait_recv()
        out[...] = (keep[n] + gprecv[n].astype(F32)).astype(BF16)

    for n in range(3):
        own_to_pair(n).wait_send()
        own_to_sib(n).wait_send()
        pair_to_sib(n).wait_send()
    for n in range(2):
        pair_copy(n).wait_send()
    for m in range(4):
        sib_copy(m).wait_send()

    def drain(t, carry):
        for k in (1, 2, 3):
            pre_copy(t, k).wait_send()
            for c in range(2):
                hid_copy(2 * t + c, k).wait_send()
                act_copy(2 * t + c, k).wait_send()
        return carry

    lax.fori_loop(0, steps, drain, 0)
    for t in range(steps - 1):
        for c in range(2):
            st_copy(t, c).wait_send()


def on_device(state_in, saved_inputs, slot_rows, combine, w_gate, w_up, w_down):
    steps, _, _, tokens, width = saved_inputs.shape
    hidden = w_gate.shape[2]
    layers = 2 * steps
    sems = pltpu.SemaphoreType.DMA
    vmem = pl.BlockSpec(memory_space=pltpu.VMEM)
    anywhere = pl.BlockSpec(memory_space=pl.ANY)
    state_out, grad_gate, grad_up = pl.pallas_call(
        relay_kernel,
        out_shape=(
            jax.ShapeDtypeStruct((2, tokens, width), BF16),
            jax.ShapeDtypeStruct((width, hidden), BF16),
            jax.ShapeDtypeStruct((width, hidden), BF16),
        ),
        in_specs=[vmem] * 4 + [anywhere] * 3,
        out_specs=(vmem, vmem, vmem),
        scratch_shapes=[
            pltpu.VMEM((layers, tokens, width), BF16),
            pltpu.VMEM((4, width, hidden), BF16),
            pltpu.VMEM((4, width, hidden), BF16),
            pltpu.VMEM((4, hidden, width), BF16),
            pltpu.VMEM((steps, 2, tokens, width), BF16),
            pltpu.VMEM((steps, 2, tokens, width), BF16),
            pltpu.VMEM((steps, 4, 2, 2 * tokens, hidden), BF16),
            pltpu.VMEM((steps, 3, 2, 2 * tokens, hidden), BF16),
            pltpu.VMEM((2, 2 * tokens, hidden), F32),
            pltpu.VMEM((layers, 4, tokens, hidden), BF16),
            pltpu.VMEM((layers, 3, tokens, hidden), BF16),
            pltpu.VMEM((layers, 4, 2, tokens, hidden), BF16),
            pltpu.VMEM((4, width, hidden), BF16),
            pltpu.VMEM((4, width, hidden), BF16),
            pltpu.VMEM((2, width, hidden), BF16),
            pltpu.VMEM((2, width, hidden), BF16),
            pltpu.VMEM((2, width, hidden), F32),
            sems((3,)), sems((3,)), sems((3,)), sems((3,)), sems((3,)), sems((3,)), sems((3,)),
            sems((steps, 3)), sems((steps, 3)),
            sems((layers, 3)), sems((layers, 3)),
            sems((layers, 3)), sems((layers, 3)),
            sems((steps - 1, 2)), sems((steps - 1, 2)),
            sems((4,)), sems((4,)), sems((2,)), sems((2,)),
        ],
        compiler_params=pltpu.CompilerParams(
            collective_id=0, has_side_effects=True, vmem_limit_bytes=56 * 2**20
        ),
        cost_estimate=pl.CostEstimate(
            flops=2 * layers * tokens * width * 4 * hidden * 7,
            bytes_accessed=2 * (layers * tokens * width + 5 * width * hidden),
            transcendentals=layers * tokens * hidden,
        ),
        name="relay",
    )(
        state_in[:, 0],
        saved_inputs.reshape(layers, tokens, width),
        slot_rows.reshape(layers, 1, tokens),
        combine.reshape(layers, 1, tokens),
        w_gate[0],
        w_up[0],
        w_down[0],
    )
    return state_out[:, None], grad_gate[None], grad_up[None]


def solution(mesh):
    placed = (
        P(None, "section", "dp", "expert"),
        P(None, None, "section", "dp", "expert"),
        P(None, None, "section", "dp"),
        P(None, None, "section", "dp"),
        P("section", "expert", "dp"),
        P("section", "expert", "dp"),
        P("section", "dp", "expert"),
    )
    return jax.shard_map(
        on_device,
        mesh=mesh,
        in_specs=placed,
        out_specs=(
            P(None, "section", "dp", "expert"),
            P("section", "expert", "dp"),
            P("section", "expert", "dp"),
        ),
        check_vma=False,
    )
```

```python
import jax
import jax.numpy as jnp
from jax import lax
from jax.experimental import pallas as pl
from jax.experimental.pallas import tpu as pltpu
from jax.sharding import PartitionSpec as P

MESH = pl.DeviceIdType.MESH
F32 = jnp.float32
BF16 = jnp.bfloat16


def dot_nn(a, b):
    return lax.dot_general(a, b, (((1,), (0,)), ((), ())), preferred_element_type=F32)


def dot_nt(a, b):
    return lax.dot_general(a, b, (((1,), (1,)), ((), ())), preferred_element_type=F32)


def dot_tn(a, b):
    return lax.dot_general(a, b, (((0,), (0,)), ((), ())), preferred_element_type=F32)


def relay_kernel(
    state_ref, x_ref, rows_ref, comb_ref, wg_ref, wu_ref, wd_ref,
    state_out, gg_out, gu_out,
    xs, wga, wua, wda, st, sn, ppart, via, precv, ab, hpart, hrecv, act,
    gsend, grecv, psend, gprecv, keep, xlate, actlate,
    loc_sem, ws_send, ws_recv, wp_send, wp_recv, wf_send, wf_recv,
    pre_s, pre_r, hid_s, hid_r, act_s, act_r, fwd_s, fwd_r, st_s, st_r,
    gs_s, gs_r, gp_s, gp_r, xl_s, xl_r, al_s, al_r,
):
    s = lax.axis_index("section")
    e = lax.axis_index("expert")
    p = lax.axis_index("dp")
    sections = lax.axis_size("section")
    steps = st.shape[0]
    tokens = st.shape[2]
    sib = p + 1 - 2 * lax.rem(p, 2)
    pair = lax.rem(p + 2, 4)
    diag = lax.rem(sib + 2, 4)
    sib_dev = (s, e, sib)
    pair_dev = (s, e, pair)
    diag_dev = (s, e, diag)
    ahead, across, behind = (lax.rem(e + k, 4) for k in (1, 2, 3))
    ahead_dev = (s, ahead, p)
    behind_dev = (s, behind, p)
    below = (lax.rem(s + sections - 1, sections), e, p)
    above = (lax.rem(s + 1, sections), e, p)

    def peer(k):
        return lax.rem(e + k, 4)

    def peer_dev(k):
        return (s, peer(k), p)

    def remote(src, dst, send, recv, dev):
        return pltpu.make_async_remote_copy(
            src_ref=src, dst_ref=dst, send_sem=send, recv_sem=recv,
            device_id=dev, device_id_type=MESH,
        )

    barrier = pltpu.get_barrier_semaphore()
    for dev in (peer_dev(1), peer_dev(2), peer_dev(3), sib_dev, pair_dev, diag_dev, below, above):
        pl.semaphore_signal(barrier, inc=1, device_id=dev, device_id_type=MESH)
    pl.semaphore_wait(barrier, 8)

    weights = ((wg_ref, wga), (wu_ref, wua), (wd_ref, wda))

    def own_to_pair(n):
        src, dst = weights[n]
        return remote(src, dst.at[p], wp_send.at[n], wp_recv.at[n], pair_dev)

    def own_to_sib(n):
        src, dst = weights[n]
        return remote(src, dst.at[p], ws_send.at[n], ws_recv.at[n], sib_dev)

    def pair_to_sib(n):
        dst = weights[n][1]
        return remote(dst.at[pair], dst.at[pair], wf_send.at[n], wf_recv.at[n], sib_dev)

    def local(n):
        src, dst = weights[n]
        return pltpu.make_async_copy(src, dst.at[p], loc_sem.at[n])

    for n in range(3):
        own_to_pair(n).start()
    for n in range(3):
        own_to_sib(n).start()
        local(n).start()

    def chosen(i):
        token = lax.broadcasted_iota(jnp.int32, (tokens, tokens), 0)
        return token == rows_ref[i]

    def sort_rows(i, carry):
        pick = jnp.where(chosen(i), 1.0, 0.0).astype(BF16)
        xs[i] = dot_nn(pick, x_ref[i]).astype(BF16)
        return carry

    lax.fori_loop(0, 2 * steps, sort_rows, 0)
    st[0] = state_ref[...]

    def pre_chunk(t, q):
        x = xs[pl.ds(2 * t, 2)].reshape(2 * tokens, xs.shape[2])
        ppart[t, q, 0] = dot_nn(x, wga[q]).astype(BF16)
        ppart[t, q, 1] = dot_nn(x, wua[q]).astype(BF16)

    def pre_copy(t, m):
        src, dst, dev = (
            (ppart.at[t, across, 0], via.at[t, 0], ahead_dev),
            (ppart.at[t, across, 1], via.at[t, 1], behind_dev),
            (ppart.at[t, ahead, 1], precv.at[t, 0], ahead_dev),
            (ppart.at[t, behind, 0], precv.at[t, 1], behind_dev),
            (ppart.at[t, ahead, 0], precv.at[t, 2], ahead_dev),
            (ppart.at[t, behind, 1], precv.at[t, 3], behind_dev),
        )[m]
        return remote(src, dst, pre_s.at[t, m], pre_r.at[t, m], dev)

    def pre_first(t):
        for m in range(4):
            pre_copy(t, m).start()

    def pre_second(t):
        pre_copy(t, 0).wait_recv()
        ppart[t, ahead, 0] = (ppart[t, ahead, 0].astype(F32) + via[t, 0].astype(F32)).astype(BF16)
        pre_copy(t, 4).start()
        pre_copy(t, 1).wait_recv()
        ppart[t, behind, 1] = (ppart[t, behind, 1].astype(F32) + via[t, 1].astype(F32)).astype(BF16)
        pre_copy(t, 5).start()

    local(0).wait()
    local(1).wait()
    pre_chunk(0, p)
    own_to_sib(0).wait_recv()
    own_to_sib(1).wait_recv()
    pre_chunk(0, sib)
    own_to_pair(0).wait_recv()
    pair_to_sib(0).start()
    own_to_pair(1).wait_recv()
    pair_to_sib(1).start()
    pre_chunk(0, pair)
    pair_to_sib(0).wait_recv()
    pair_to_sib(1).wait_recv()
    pre_chunk(0, diag)
    pre_first(0)
    pre_second(0)
    local(2).wait()
    own_to_pair(2).wait_recv()
    pair_to_sib(2).start()
    own_to_sib(2).wait_recv()
    pair_to_sib(2).wait_recv()

    def hid_copy(i, k):
        return remote(hpart.at[i, peer(k)], hrecv.at[i, k - 1], hid_s.at[i, k - 1], hid_r.at[i, k - 1], peer_dev(k))

    def act_copy(i, way):
        return remote(act.at[i, e], act.at[i, e], act_s.at[i, way], act_r.at[i, way], (ahead_dev, behind_dev)[way])

    def act_arrival(i, way):
        there = (behind, ahead)[way]
        return remote(
            act.at[i, there], act.at[i, there], act_s.at[i, way], act_r.at[i, way], (ahead_dev, behind_dev)[way]
        )

    def act_forward(i, way):
        there = (behind, ahead)[way]
        return remote(
            act.at[i, there, way], act.at[i, there, way], fwd_s.at[i, way], fwd_r.at[i, way],
            (ahead_dev, behind_dev)[way],
        )

    def act_last(i, way):
        return remote(
            act.at[i, across, way], act.at[i, across, way], fwd_s.at[i, way], fwd_r.at[i, way],
            (ahead_dev, behind_dev)[way],
        )

    def pass_on(i):
        for way in range(2):
            act_arrival(i, way).wait_recv()
            act_forward(i, way).start()

    early = 2 * (steps - 1)

    def weight_grad(q, n, layers):
        rows = xs[0:layers].reshape(layers * tokens, xs.shape[2])
        grads = act[0:layers, q, n].reshape(layers * tokens, act.shape[4])
        return dot_tn(rows, grads)

    def sib_copy(m):
        return remote(gsend.at[m], grecv.at[m], gs_s.at[m], gs_r.at[m], sib_dev)

    def pair_copy(n):
        return remote(psend.at[n], gprecv.at[n], gp_s.at[n], gp_r.at[n], pair_dev)

    def rows_copy(m):
        src, dst, dev = (
            (xs.at[pl.ds(early, 2)], xlate.at[p], sib_dev),
            (xs.at[pl.ds(early, 2)], xlate.at[p], pair_dev),
            (xlate.at[pair], xlate.at[pair], sib_dev),
        )[m]
        return remote(src, dst, xl_s.at[m], xl_r.at[m], dev)

    def late_copy(c, m):
        there, dev = ((sib, sib_dev), (pair, pair_dev), (diag, diag_dev))[m]
        return remote(act.at[early + c, there], actlate.at[p, c], al_s.at[c, m], al_r.at[c, m], dev)

    def st_copy(t, c):
        return remote(sn.at[t, c], st.at[t + 1, c], st_s.at[t, c], st_r.at[t, c], below if c == 0 else above)

    def step(t, carry):
        for c in range(2):
            i = 2 * t + c

            @pl.when(t > 0)
            def _():
                st_copy(t - 1, c).wait_recv()

            weight = jnp.sum(jnp.where(chosen(i), comb_ref[i], 0.0), axis=1, keepdims=True)
            slot_grads = (weight * st[t, c].astype(F32)).astype(BF16)
            for q in range(4):
                hpart[i, q] = dot_nt(slot_grads, wda[q]).astype(BF16)
            for k in (2, 1, 3):
                hid_copy(i, k).start()

        for m in range(2, 6):
            pre_copy(t, m).wait_recv()
        pre_gate = ppart[t, e, 0].astype(F32) + precv[t, 1].astype(F32) + precv[t, 2].astype(F32)
        pre_up = ppart[t, e, 1].astype(F32) + precv[t, 0].astype(F32) + precv[t, 3].astype(F32)
        sigma = jax.nn.sigmoid(pre_gate)
        ab[0] = pre_up * sigma * (1.0 + pre_gate * (1.0 - sigma))
        ab[1] = pre_gate * sigma

        for c in range(2):
            i = 2 * t + c
            for k in (1, 3, 2):
                hid_copy(i, k).wait_recv()
            hidden = hpart[i, e].astype(F32)
            for k in range(3):
                hidden += hrecv[i, k].astype(F32)
            act[i, e, 0] = (hidden * ab[0, c * tokens:(c + 1) * tokens]).astype(BF16)
            act[i, e, 1] = (hidden * ab[1, c * tokens:(c + 1) * tokens]).astype(BF16)
            for way in range(2):
                act_copy(i, way).start()

        @pl.when(t < steps - 1)
        def _():
            for q in range(4):
                pre_chunk(t + 1, q)
                if q == 1:
                    pass_on(2 * t)
            pass_on(2 * t + 1)
            pre_first(t + 1)

        @pl.when(t == steps - 1)
        def _():
            rows_copy(1).start()
            rows_copy(0).start()
            for n in range(2):
                gsend[n] = weight_grad(diag, n, early).astype(BF16)
                sib_copy(n).start()
            pass_on(2 * t)
            for n in range(2):
                keep[n] = weight_grad(pair, n, early)
            pass_on(2 * t + 1)
            for n in range(2):
                sib_copy(n).wait_recv()
                psend[n] = (keep[n] + grecv[n].astype(F32)).astype(BF16)
                pair_copy(n).start()

        for c in range(2):
            i = 2 * t + c
            total = st[t, c].astype(F32)
            for q in (e, behind, ahead):
                total += dot_nt(act[i, q, 0], wga[q]) + dot_nt(act[i, q, 1], wua[q])
            for way in range(2):
                act_last(i, way).wait_recv()

            @pl.when(t == steps - 1)
            def _():
                for m in (2, 1, 0):
                    late_copy(c, m).start()

            total += dot_nt(act[i, across, 0], wga[across]) + dot_nt(act[i, across, 1], wua[across])
            sn[t, c] = total.astype(BF16)

            @pl.when(t < steps - 1)
            def _():
                st_copy(t, c).start()

        @pl.when(t < steps - 1)
        def _():
            pre_second(t + 1)

        return carry

    lax.fori_loop(0, steps, step, 0)
    state_out[...] = sn[steps - 1]

    for n in range(2):
        gsend[2 + n] = weight_grad(sib, n, early).astype(BF16)
        sib_copy(2 + n).start()
    rows_copy(1).wait_recv()
    rows_copy(2).start()
    for n in range(2):
        keep[n] = weight_grad(p, n, 2 * steps)

    def add_late(there, m):
        for c in range(2):
            late_copy(c, m).wait_recv()
        rows = xlate[there].reshape(2 * tokens, xs.shape[2])
        for n in range(2):
            keep[n] += dot_tn(rows, actlate[there, :, n].reshape(2 * tokens, act.shape[4]))

    rows_copy(0).wait_recv()
    add_late(sib, 0)
    for n in range(2):
        sib_copy(2 + n).wait_recv()
        keep[n] += grecv[2 + n].astype(F32)
    add_late(pair, 1)
    rows_copy(2).wait_recv()
    add_late(diag, 2)
    for n, out in ((0, gg_out), (1, gu_out)):
        pair_copy(n).wait_recv()
        out[...] = (keep[n] + gprecv[n].astype(F32)).astype(BF16)

    for n in range(3):
        own_to_pair(n).wait_send()
        own_to_sib(n).wait_send()
        pair_to_sib(n).wait_send()
    for n in range(2):
        pair_copy(n).wait_send()
    for m in range(4):
        sib_copy(m).wait_send()
    for m in range(3):
        rows_copy(m).wait_send()
        for c in range(2):
            late_copy(c, m).wait_send()

    def drain(t, carry):
        for m in range(6):
            pre_copy(t, m).wait_send()
        for c in range(2):
            for k in (1, 2, 3):
                hid_copy(2 * t + c, k).wait_send()
            for way in range(2):
                act_copy(2 * t + c, way).wait_send()
                act_forward(2 * t + c, way).wait_send()
        return carry

    lax.fori_loop(0, steps, drain, 0)
    for t in range(steps - 1):
        for c in range(2):
            st_copy(t, c).wait_send()


def on_device(state_in, saved_inputs, slot_rows, combine, w_gate, w_up, w_down):
    steps, _, _, tokens, width = saved_inputs.shape
    hidden = w_gate.shape[2]
    layers = 2 * steps
    sems = pltpu.SemaphoreType.DMA
    vmem = pl.BlockSpec(memory_space=pltpu.VMEM)
    anywhere = pl.BlockSpec(memory_space=pl.ANY)
    state_out, grad_gate, grad_up = pl.pallas_call(
        relay_kernel,
        out_shape=(
            jax.ShapeDtypeStruct((2, tokens, width), BF16),
            jax.ShapeDtypeStruct((width, hidden), BF16),
            jax.ShapeDtypeStruct((width, hidden), BF16),
        ),
        in_specs=[vmem] * 4 + [anywhere] * 3,
        out_specs=(vmem, vmem, vmem),
        scratch_shapes=[
            pltpu.VMEM((layers, tokens, width), BF16),
            pltpu.VMEM((4, width, hidden), BF16),
            pltpu.VMEM((4, width, hidden), BF16),
            pltpu.VMEM((4, hidden, width), BF16),
            pltpu.VMEM((steps, 2, tokens, width), BF16),
            pltpu.VMEM((steps, 2, tokens, width), BF16),
            pltpu.VMEM((steps, 4, 2, 2 * tokens, hidden), BF16),
            pltpu.VMEM((steps, 2, 2 * tokens, hidden), BF16),
            pltpu.VMEM((steps, 4, 2 * tokens, hidden), BF16),
            pltpu.VMEM((2, 2 * tokens, hidden), F32),
            pltpu.VMEM((layers, 4, tokens, hidden), BF16),
            pltpu.VMEM((layers, 3, tokens, hidden), BF16),
            pltpu.VMEM((layers, 4, 2, tokens, hidden), BF16),
            pltpu.VMEM((4, width, hidden), BF16),
            pltpu.VMEM((4, width, hidden), BF16),
            pltpu.VMEM((2, width, hidden), BF16),
            pltpu.VMEM((2, width, hidden), BF16),
            pltpu.VMEM((2, width, hidden), F32),
            pltpu.VMEM((4, 2, tokens, width), BF16),
            pltpu.VMEM((4, 2, 2, tokens, hidden), BF16),
            sems((3,)), sems((3,)), sems((3,)), sems((3,)), sems((3,)), sems((3,)), sems((3,)),
            sems((steps, 6)), sems((steps, 6)),
            sems((layers, 3)), sems((layers, 3)),
            sems((layers, 2)), sems((layers, 2)),
            sems((layers, 2)), sems((layers, 2)),
            sems((steps - 1, 2)), sems((steps - 1, 2)),
            sems((4,)), sems((4,)), sems((2,)), sems((2,)),
            sems((3,)), sems((3,)), sems((2, 3)), sems((2, 3)),
        ],
        compiler_params=pltpu.CompilerParams(
            collective_id=0, has_side_effects=True, vmem_limit_bytes=56 * 2**20
        ),
        cost_estimate=pl.CostEstimate(
            flops=2 * layers * tokens * width * 4 * hidden * 7,
            bytes_accessed=2 * (layers * tokens * width + 5 * width * hidden),
            transcendentals=layers * tokens * hidden,
        ),
        name="relay",
    )(
        state_in[:, 0],
        saved_inputs.reshape(layers, tokens, width),
        slot_rows.reshape(layers, 1, tokens),
        combine.reshape(layers, 1, tokens),
        w_gate[0],
        w_up[0],
        w_down[0],
    )
    return state_out[:, None], grad_gate[None], grad_up[None]


def solution(mesh):
    placed = (
        P(None, "section", "dp", "expert"),
        P(None, None, "section", "dp", "expert"),
        P(None, None, "section", "dp"),
        P(None, None, "section", "dp"),
        P("section", "expert", "dp"),
        P("section", "expert", "dp"),
        P("section", "dp", "expert"),
    )
    return jax.shard_map(
        on_device,
        mesh=mesh,
        in_specs=placed,
        out_specs=(
            P(None, "section", "dp", "expert"),
            P("section", "expert", "dp"),
            P("section", "expert", "dp"),
        ),
        check_vma=False,
    )
```

```python
import jax
import jax.numpy as jnp
from jax import lax
from jax.experimental import pallas as pl
from jax.experimental.pallas import tpu as pltpu
from jax.sharding import PartitionSpec as P

MESH = pl.DeviceIdType.MESH
F32 = jnp.float32
BF16 = jnp.bfloat16


def dot_nn(a, b):
    return lax.dot_general(a, b, (((1,), (0,)), ((), ())), preferred_element_type=F32)


def dot_nt(a, b):
    return lax.dot_general(a, b, (((1,), (1,)), ((), ())), preferred_element_type=F32)


def dot_tn(a, b):
    return lax.dot_general(a, b, (((0,), (0,)), ((), ())), preferred_element_type=F32)


def relay_kernel(
    state_ref, x_ref, rows_ref, comb_ref, wg_ref, wu_ref, wd_ref,
    state_out, gg_out, gu_out,
    xraw, xhome, rows, comb, xs, wga, wua, wda, st, sn, back, ppart, via, precv, ab, hpart, hvia, hrecv, act,
    actlate, keep,
    loc_sem, home_sem, ws_send, ws_recv, wp_send, wp_recv, wf_send, wf_recv, in_s, in_r,
    pre_s, pre_r, hid_s, hid_r, act_s, act_r, st_s, st_r, back_s, back_r, xl_s, xl_r, al_s, al_r,
):
    s = lax.axis_index("section")
    e = lax.axis_index("expert")
    p = lax.axis_index("dp")
    sections = lax.axis_size("section")
    steps = st.shape[0]
    tokens = st.shape[2]
    core = lax.rem(p, 2)
    low = lax.div(p, 2)
    sib = p + 1 - 2 * core
    pair = lax.rem(p + 2, 4)
    diag = lax.rem(sib + 2, 4)
    sib_dev = (s, e, sib)
    pair_dev = (s, e, pair)
    diag_dev = (s, e, diag)
    below = (lax.rem(s + sections - 1, sections), e, p)
    above = (lax.rem(s + 1, sections), e, p)

    swapped = lax.rem(e + core, 2) == 1
    near = lax.rem(e + 3 + 2 * low, 4)
    far = lax.rem(e + 1 + 2 * low, 4)
    oppo = lax.rem(e + 2, 4)
    near_dev = (s, near, pair)
    far_dev = (s, far, pair)
    oppo_dev = (s, oppo, p)

    def remote(src, dst, send, recv, dev):
        return pltpu.make_async_remote_copy(
            src_ref=src, dst_ref=dst, send_sem=send, recv_sem=recv,
            device_id=dev, device_id_type=MESH,
        )

    barrier = pltpu.get_barrier_semaphore()
    for dev in (near_dev, far_dev, oppo_dev, sib_dev, pair_dev, diag_dev, below, above):
        pl.semaphore_signal(barrier, inc=1, device_id=dev, device_id_type=MESH)
    pl.semaphore_wait(barrier, 8)

    def input_refs(m):
        if m == 0:
            return state_ref, st.at[0]
        if m == 1:
            return rows_ref, rows
        if m == 2:
            return comb_ref, comb
        return x_ref.at[pl.ds(2 * (m - 3), 2)], xraw.at[pl.ds(2 * (m - 3), 2)]

    def swap_copy(m):
        src, dst = input_refs(m)
        return remote(src, dst, in_s.at[m], in_r.at[m], pair_dev)

    def stay_copy(m):
        src, dst = input_refs(m)
        return pltpu.make_async_copy(src, dst, in_r.at[m])

    def input_start(members):
        @pl.when(swapped)
        def _():
            for m in members:
                swap_copy(m).start()

        @pl.when(jnp.logical_not(swapped))
        def _():
            for m in members:
                stay_copy(m).start()

    def input_wait(members):
        @pl.when(swapped)
        def _():
            for m in members:
                swap_copy(m).wait_recv()

        @pl.when(jnp.logical_not(swapped))
        def _():
            for m in members:
                stay_copy(m).wait()

    def weight_refs(n):
        src, dst = ((wg_ref, wga), (wu_ref, wua), (wd_ref, wda))[n // 2]
        depth = src.shape[0] // 2
        return src, dst, pl.ds((n % 2) * depth, depth)

    def own_to_pair(n):
        src, dst, part = weight_refs(n)
        return remote(src.at[part], dst.at[p, part], wp_send.at[n], wp_recv.at[n], pair_dev)

    def own_to_sib(n):
        src, dst, part = weight_refs(n)
        return remote(src.at[part], dst.at[p, part], ws_send.at[n], ws_recv.at[n], sib_dev)

    def pair_to_sib(n):
        src, dst, part = weight_refs(n)
        return remote(dst.at[pair, part], dst.at[pair, part], wf_send.at[n], wf_recv.at[n], sib_dev)

    def local(n):
        src, dst, part = weight_refs(n)
        return pltpu.make_async_copy(src.at[part], dst.at[p, part], loc_sem.at[n])

    def forward(n):
        own_to_pair(n).wait_recv()
        pair_to_sib(n).start()
        if n + 3 < 6:
            own_to_pair(n + 3).start()

    home = pltpu.make_async_copy(x_ref, xhome, home_sem.at[0])

    input_start((1, 2, 3))
    for n in range(3):
        own_to_pair(n).start()
    for n in range(6):
        local(n).start()
        own_to_sib(n).start()
    home.start()

    def chosen(of, i):
        token = lax.broadcasted_iota(jnp.int32, (tokens, tokens), 0)
        return token == of[i]

    def sort_rows(t, of, raw, there):
        for c in range(2):
            i = 2 * t + c
            pick = jnp.where(chosen(of, i), 1.0, 0.0).astype(BF16)
            xs[there, i] = dot_nn(pick, raw[i]).astype(BF16)

    def pre_chunk(t, q):
        x = xs[p, pl.ds(2 * t, 2)].reshape(2 * tokens, xs.shape[3])
        ppart[t, q, 0] = dot_nn(x, wga[q]).astype(BF16)
        ppart[t, q, 1] = dot_nn(x, wua[q]).astype(BF16)

    def pre_copy(t, m):
        src, dst, dev = (
            (ppart.at[t, near], via.at[t, 0], near_dev),
            (ppart.at[t, oppo], via.at[t, 1], near_dev),
            (ppart.at[t, far], precv.at[t], far_dev),
        )[m]
        return remote(src, dst, pre_s.at[t, m], pre_r.at[t, m], dev)

    def pre_second(t):
        pre_copy(t, 1).wait_recv()
        for n in range(2):
            ppart[t, far, n] = (ppart[t, far, n].astype(F32) + via[t, 1, n].astype(F32)).astype(BF16)
        pre_copy(t, 2).start()

    def rows_copy(t, m):
        there, dev = ((p, sib_dev), (p, pair_dev), (pair, sib_dev))[m]
        part = pl.ds(2 * t, 2)
        return remote(xs.at[there, part], xs.at[there, part], xl_s.at[t, m], xl_r.at[t, m], dev)

    def rows_first(t):
        rows_copy(t, 0).start()

        @pl.when(jnp.logical_not(swapped))
        def _():
            rows_copy(t, 1).start()

    def rows_second(t):
        @pl.when(swapped)
        def _():
            sort_rows(t, rows_ref, xhome, pair)

        @pl.when(jnp.logical_not(swapped))
        def _():
            there, part = pair, pl.ds(2 * t, 2)
            remote(
                xs.at[there, part], xs.at[there, part], xl_s.at[t, 1], xl_r.at[t, 1], pair_dev
            ).wait_recv()

        rows_copy(t, 2).start()

    input_wait((1, 2, 3))
    sort_rows(0, rows, xraw, p)
    for n in range(4):
        local(n).wait()
    pre_chunk(0, p)
    forward(0)
    for n in range(4):
        own_to_sib(n).wait_recv()
    pre_chunk(0, sib)
    for n in range(1, 4):
        forward(n)
    input_start((0,))
    pre_chunk(0, pair)
    for n in range(4):
        pair_to_sib(n).wait_recv()
    pre_chunk(0, diag)
    pre_copy(0, 1).start()
    pre_copy(0, 0).start()
    home.wait()
    forward(4)
    for n in (4, 5):
        local(n).wait()
        own_to_sib(n).wait_recv()
    forward(5)
    pre_second(0)
    input_start((4,))
    rows_first(0)
    input_wait((0,))

    def hid_copy(i, m):
        src, dst, dev = (
            (hpart.at[i, near], hvia.at[i, 0], near_dev),
            (hpart.at[i, oppo], hvia.at[i, 1], near_dev),
            (hpart.at[i, far], hrecv.at[i], far_dev),
        )[m]
        return remote(src, dst, hid_s.at[i, m], hid_r.at[i, m], dev)

    def act_copy(i, m):
        q, dev = ((e, near_dev), (e, far_dev), (far, near_dev))[m]
        return remote(act.at[i, q], act.at[i, q], act_s.at[i, m], act_r.at[i, m], dev)

    def act_arrival(i, m):
        q, dev = ((near, near_dev), (far, far_dev), (oppo, near_dev))[m]
        return remote(act.at[i, q], act.at[i, q], act_s.at[i, m], act_r.at[i, m], dev)

    def pass_on(i):
        act_arrival(i, 1).wait_recv()
        act_copy(i, 2).start()

    def late_copy(i, m):
        there, dev = ((sib, sib_dev), (pair, pair_dev), (diag, diag_dev))[m]
        return remote(act.at[i, there], actlate.at[p, i], al_s.at[i, m], al_r.at[i, m], dev)

    def weight_grad(there, grads, first, layers):
        flat = xs[there, first:first + layers].reshape(layers * tokens, xs.shape[3])
        return [
            dot_tn(flat, grads[first:first + layers, n].reshape(layers * tokens, act.shape[4])) for n in range(2)
        ]

    def add_others(there, m, first, layers):
        for i in range(first, first + layers):
            late_copy(i, m).wait_recv()
        for n, grad in enumerate(weight_grad(there, actlate.at[there], first, layers)):
            keep[n] += grad

    def rows_arrive(t, m):
        there, part = ((sib, diag)[m // 2], pl.ds(2 * t, 2))
        remote(xs.at[there, part], xs.at[there, part], xl_s.at[t, m], xl_r.at[t, m], sib_dev).wait_recv()

    early = 2 * (steps - 1)

    def st_copy(t, c):
        return remote(sn.at[t, c], st.at[t + 1, c], st_s.at[t, c], st_r.at[t, c], below if c == 0 else above)

    def back_copy(c):
        return remote(sn.at[steps - 1, c], back.at[c], back_s.at[c], back_r.at[c], pair_dev)

    def step(t, carry):
        for c in range(2):
            i = 2 * t + c

            @pl.when(t > 0)
            def _():
                st_copy(t - 1, c).wait_recv()

            weight = jnp.sum(jnp.where(chosen(rows, i), comb[i], 0.0), axis=1, keepdims=True)
            slot_grads = (weight * st[t, c].astype(F32)).astype(BF16)
            if c == 0:
                @pl.when(t == 0)
                def _():
                    for n in (4, 5):
                        pair_to_sib(n).wait_recv()

            for m, q in ((1, oppo), (0, near)):
                hpart[i, q] = dot_nt(slot_grads, wda[q]).astype(BF16)
                hid_copy(i, m).start()
            for q in (far, e):
                hpart[i, q] = dot_nt(slot_grads, wda[q]).astype(BF16)

        for c in range(2):
            i = 2 * t + c
            hid_copy(i, 1).wait_recv()
            hpart[i, far] = (hpart[i, far].astype(F32) + hvia[i, 1].astype(F32)).astype(BF16)
            hid_copy(i, 2).start()

        for ahead in range(2, steps):
            @pl.when(t == ahead - 2)
            def _():
                input_start((3 + ahead,))

        pre_copy(t, 0).wait_recv()
        pre_copy(t, 2).wait_recv()
        pre_gate, pre_up = (
            ppart[t, e, n].astype(F32) + via[t, 0, n].astype(F32) + precv[t, n].astype(F32) for n in range(2)
        )
        sigma = jax.nn.sigmoid(pre_gate)
        ab[0] = pre_up * sigma * (1.0 + pre_gate * (1.0 - sigma))
        ab[1] = pre_gate * sigma

        for c in range(2):
            i = 2 * t + c
            for m in (0, 2):
                hid_copy(i, m).wait_recv()
            hidden = hpart[i, e].astype(F32) + hvia[i, 0].astype(F32) + hrecv[i].astype(F32)
            act[i, e, 0] = (hidden * ab[0, c * tokens:(c + 1) * tokens]).astype(BF16)
            act[i, e, 1] = (hidden * ab[1, c * tokens:(c + 1) * tokens]).astype(BF16)
            act_copy(i, 1).start()
            act_copy(i, 0).start()

        rows_second(t)
        for ahead in range(1, steps):
            @pl.when(t == ahead - 1)
            def _():
                input_wait((3 + ahead,))

        @pl.when(t < steps - 1)
        def _():
            sort_rows(t + 1, rows, xraw, p)
            pre_chunk(t + 1, oppo)
            pre_chunk(t + 1, near)
            pass_on(2 * t)
            pre_chunk(t + 1, far)
            pass_on(2 * t + 1)
            pre_copy(t + 1, 1).start()
            pre_copy(t + 1, 0).start()
            pre_chunk(t + 1, e)

        @pl.when(t == steps - 1)
        def _():
            for n, grad in enumerate(weight_grad(p, act.at[:, p], 0, early)):
                keep[n] = grad
            pass_on(2 * t)
            for ahead in range(steps - 1):
                rows_arrive(ahead, 0)
            add_others(sib, 0, 0, early)
            pass_on(2 * t + 1)
            add_others(pair, 1, 0, early)
            for ahead in range(steps - 1):
                rows_arrive(ahead, 2)
            add_others(diag, 2, 0, early)

        for c in range(2):
            i = 2 * t + c
            total = st[t, c].astype(F32)
            for q in (e, far, near):
                if q is near:
                    act_arrival(i, 0).wait_recv()
                total += dot_nt(act[i, q, 0], wga[q]) + dot_nt(act[i, q, 1], wua[q])
            act_arrival(i, 2).wait_recv()

            total += dot_nt(act[i, oppo, 0], wga[oppo]) + dot_nt(act[i, oppo, 1], wua[oppo])
            sn[t, c] = total.astype(BF16)

            @pl.when(t < steps - 1)
            def _():
                st_copy(t, c).start()

            for m in (2, 1, 0):
                late_copy(i, m).start()

        @pl.when(t < steps - 1)
        def _():
            pre_second(t + 1)
            rows_first(t + 1)

        return carry

    lax.fori_loop(0, steps, step, 0)

    @pl.when(swapped)
    def _():
        for c in range(2):
            back_copy(c).start()

    for n, grad in enumerate(weight_grad(p, act.at[:, p], early, 2)):
        keep[n] += grad
    rows_arrive(steps - 1, 0)
    add_others(sib, 0, early, 2)
    rows_arrive(steps - 1, 2)
    add_others(diag, 2, early, 2)
    add_others(pair, 1, early, 2)
    for n, out in ((0, gg_out), (1, gu_out)):
        out[...] = keep[n].astype(BF16)

    @pl.when(swapped)
    def _():
        for c in range(2):
            back_copy(c).wait_recv()
            state_out[c] = back[c]

    @pl.when(jnp.logical_not(swapped))
    def _():
        state_out[...] = sn[steps - 1]

    @pl.when(swapped)
    def _():
        for m in range(3 + steps):
            swap_copy(m).wait_send()
        for c in range(2):
            back_copy(c).wait_send()

    for n in range(6):
        own_to_pair(n).wait_send()
        own_to_sib(n).wait_send()
        pair_to_sib(n).wait_send()
    def drain(t, carry):
        for m in range(3):
            pre_copy(t, m).wait_send()
            for c in range(2):
                hid_copy(2 * t + c, m).wait_send()
                act_copy(2 * t + c, m).wait_send()
                late_copy(2 * t + c, m).wait_send()
        rows_copy(t, 0).wait_send()
        rows_copy(t, 2).wait_send()

        @pl.when(jnp.logical_not(swapped))
        def _():
            rows_copy(t, 1).wait_send()

        return carry

    lax.fori_loop(0, steps, drain, 0)
    for t in range(steps - 1):
        for c in range(2):
            st_copy(t, c).wait_send()


def on_device(state_in, saved_inputs, slot_rows, combine, w_gate, w_up, w_down):
    steps, _, _, tokens, width = saved_inputs.shape
    hidden = w_gate.shape[2]
    layers = 2 * steps
    sems = pltpu.SemaphoreType.DMA
    vmem = pl.BlockSpec(memory_space=pltpu.VMEM)
    anywhere = pl.BlockSpec(memory_space=pl.ANY)
    state_out, grad_gate, grad_up = pl.pallas_call(
        relay_kernel,
        out_shape=(
            jax.ShapeDtypeStruct((2, tokens, width), BF16),
            jax.ShapeDtypeStruct((width, hidden), BF16),
            jax.ShapeDtypeStruct((width, hidden), BF16),
        ),
        in_specs=[anywhere, anywhere, vmem, vmem] + [anywhere] * 3,
        out_specs=(vmem, vmem, vmem),
        scratch_shapes=[
            pltpu.VMEM((layers, tokens, width), BF16),
            pltpu.VMEM((layers, tokens, width), BF16),
            pltpu.VMEM((layers, 1, tokens), jnp.int32),
            pltpu.VMEM((layers, 1, tokens), F32),
            pltpu.VMEM((4, layers, tokens, width), BF16),
            pltpu.VMEM((4, width, hidden), BF16),
            pltpu.VMEM((4, width, hidden), BF16),
            pltpu.VMEM((4, hidden, width), BF16),
            pltpu.VMEM((steps, 2, tokens, width), BF16),
            pltpu.VMEM((steps, 2, tokens, width), BF16),
            pltpu.VMEM((2, tokens, width), BF16),
            pltpu.VMEM((steps, 4, 2, 2 * tokens, hidden), BF16),
            pltpu.VMEM((steps, 2, 2, 2 * tokens, hidden), BF16),
            pltpu.VMEM((steps, 2, 2 * tokens, hidden), BF16),
            pltpu.VMEM((2, 2 * tokens, hidden), F32),
            pltpu.VMEM((layers, 4, tokens, hidden), BF16),
            pltpu.VMEM((layers, 2, tokens, hidden), BF16),
            pltpu.VMEM((layers, tokens, hidden), BF16),
            pltpu.VMEM((layers, 4, 2, tokens, hidden), BF16),
            pltpu.VMEM((4, layers, 2, tokens, hidden), BF16),
            pltpu.VMEM((2, width, hidden), F32),
            sems((6,)), sems((1,)), sems((6,)), sems((6,)), sems((6,)), sems((6,)), sems((6,)), sems((6,)),
            sems((3 + steps,)), sems((3 + steps,)),
            sems((steps, 3)), sems((steps, 3)),
            sems((layers, 3)), sems((layers, 3)),
            sems((layers, 3)), sems((layers, 3)),
            sems((steps - 1, 2)), sems((steps - 1, 2)),
            sems((2,)), sems((2,)),
            sems((steps, 3)), sems((steps, 3)),
            sems((layers, 3)), sems((layers, 3)),
        ],
        compiler_params=pltpu.CompilerParams(
            collective_id=0, has_side_effects=True, vmem_limit_bytes=56 * 2**20
        ),
        cost_estimate=pl.CostEstimate(
            flops=2 * layers * tokens * width * 4 * hidden * 7,
            bytes_accessed=2 * (layers * tokens * width + 5 * width * hidden),
            transcendentals=layers * tokens * hidden,
        ),
        name="relay",
    )(
        state_in[:, 0],
        saved_inputs.reshape(layers, tokens, width),
        slot_rows.reshape(layers, 1, tokens),
        combine.reshape(layers, 1, tokens),
        w_gate[0],
        w_up[0],
        w_down[0],
    )
    return state_out[:, None], grad_gate[None], grad_up[None]


def solution(mesh):
    placed = (
        P(None, "section", "dp", "expert"),
        P(None, None, "section", "dp", "expert"),
        P(None, None, "section", "dp"),
        P(None, None, "section", "dp"),
        P("section", "expert", "dp"),
        P("section", "expert", "dp"),
        P("section", "dp", "expert"),
    )
    return jax.shard_map(
        on_device,
        mesh=mesh,
        in_specs=placed,
        out_specs=(
            P(None, "section", "dp", "expert"),
            P("section", "expert", "dp"),
            P("section", "expert", "dp"),
        ),
        check_vma=False,
    )
```

```python
import jax
import jax.numpy as jnp
from jax import lax
from jax.experimental import pallas as pl
from jax.experimental.pallas import tpu as pltpu
from jax.sharding import PartitionSpec as P

MESH = pl.DeviceIdType.MESH
F32 = jnp.float32
BF16 = jnp.bfloat16


def dot_nn(a, b):
    return lax.dot_general(a, b, (((1,), (0,)), ((), ())), preferred_element_type=F32)


def dot_nt(a, b):
    return lax.dot_general(a, b, (((1,), (1,)), ((), ())), preferred_element_type=F32)


def dot_tn(a, b):
    return lax.dot_general(a, b, (((0,), (0,)), ((), ())), preferred_element_type=F32)


def relay_kernel(
    state_ref, x_ref, rows_ref, comb_ref, wg_ref, wu_ref, wd_ref,
    state_out, gg_out, gu_out,
    xraw, xhome, rows, comb, xs, wga, wua, wda, st, sn, back, ppart, via, precv, ab, hpart, hvia, hrecv, act,
    actlate, keep,
    loc_sem, home_sem, ws_send, ws_recv, wp_send, wp_recv, wf_send, wf_recv, in_s, in_r,
    pre_s, pre_r, hid_s, hid_r, act_s, act_r, st_s, st_r, back_s, back_r, xl_s, xl_r, al_s, al_r,
):
    s = lax.axis_index("section")
    e = lax.axis_index("expert")
    p = lax.axis_index("dp")
    sections = lax.axis_size("section")
    steps = st.shape[0]
    tokens = st.shape[2]
    core = lax.rem(p, 2)
    low = lax.div(p, 2)
    sib = p + 1 - 2 * core
    pair = lax.rem(p + 2, 4)
    diag = lax.rem(sib + 2, 4)
    sib_dev = (s, e, sib)
    pair_dev = (s, e, pair)
    diag_dev = (s, e, diag)
    below = (lax.rem(s + sections - 1, sections), e, p)
    above = (lax.rem(s + 1, sections), e, p)

    swapped = lax.rem(e + core, 2) == 1
    near = lax.rem(e + 3 + 2 * low, 4)
    far = lax.rem(e + 1 + 2 * low, 4)
    oppo = lax.rem(e + 2, 4)
    near_dev = (s, near, pair)
    far_dev = (s, far, pair)
    oppo_dev = (s, oppo, p)

    def remote(src, dst, send, recv, dev):
        return pltpu.make_async_remote_copy(
            src_ref=src, dst_ref=dst, send_sem=send, recv_sem=recv,
            device_id=dev, device_id_type=MESH,
        )

    barrier = pltpu.get_barrier_semaphore()
    for dev in (near_dev, far_dev, oppo_dev, sib_dev, pair_dev, diag_dev, below, above):
        pl.semaphore_signal(barrier, inc=1, device_id=dev, device_id_type=MESH)
    pl.semaphore_wait(barrier, 8)

    def input_refs(m):
        if m == 0:
            return state_ref, st.at[0]
        if m == 1:
            return rows_ref, rows
        if m == 2:
            return comb_ref, comb
        return x_ref.at[pl.ds(2 * (m - 3), 2)], xraw.at[pl.ds(2 * (m - 3), 2)]

    def swap_copy(m):
        src, dst = input_refs(m)
        return remote(src, dst, in_s.at[m], in_r.at[m], pair_dev)

    def stay_copy(m):
        src, dst = input_refs(m)
        return pltpu.make_async_copy(src, dst, in_r.at[m])

    def input_start(members):
        @pl.when(swapped)
        def _():
            for m in members:
                swap_copy(m).start()

        @pl.when(jnp.logical_not(swapped))
        def _():
            for m in members:
                stay_copy(m).start()

    def input_wait(members):
        @pl.when(swapped)
        def _():
            for m in members:
                swap_copy(m).wait_recv()

        @pl.when(jnp.logical_not(swapped))
        def _():
            for m in members:
                stay_copy(m).wait()

    def weight_refs(n):
        src, dst = ((wg_ref, wga), (wu_ref, wua), (wd_ref, wda))[n // 2]
        depth = src.shape[0] // 2
        return src, dst, pl.ds((n % 2) * depth, depth)

    def own_to_pair(n):
        src, dst, part = weight_refs(n)
        return remote(src.at[part], dst.at[p, part], wp_send.at[n], wp_recv.at[n], pair_dev)

    def own_to_sib(n):
        src, dst, part = weight_refs(n)
        return remote(src.at[part], dst.at[p, part], ws_send.at[n], ws_recv.at[n], sib_dev)

    def pair_to_sib(n):
        src, dst, part = weight_refs(n)
        return remote(dst.at[pair, part], dst.at[pair, part], wf_send.at[n], wf_recv.at[n], sib_dev)

    def local(n):
        src, dst, part = weight_refs(n)
        return pltpu.make_async_copy(src.at[part], dst.at[p, part], loc_sem.at[n])

    def forward(n):
        own_to_pair(n).wait_recv()
        pair_to_sib(n).start()
        if n + 3 < 6:
            own_to_pair(n + 3).start()

    home = pltpu.make_async_copy(x_ref, xhome, home_sem.at[0])

    input_start((1, 2, 3))
    for n in range(3):
        own_to_pair(n).start()
    for n in range(6):
        local(n).start()
        own_to_sib(n).start()
    home.start()

    def chosen(of, i):
        token = lax.broadcasted_iota(jnp.int32, (tokens, tokens), 0)
        return token == of[i]

    def sort_rows(t, of, raw, there):
        for c in range(2):
            i = 2 * t + c
            pick = jnp.where(chosen(of, i), 1.0, 0.0).astype(BF16)
            xs[there, i] = dot_nn(pick, raw[i]).astype(BF16)

    def pre_chunk(t, q):
        x = xs[p, pl.ds(2 * t, 2)].reshape(2 * tokens, xs.shape[3])
        ppart[t, q, 0] = dot_nn(x, wga[q]).astype(BF16)
        ppart[t, q, 1] = dot_nn(x, wua[q]).astype(BF16)

    def pre_copy(t, m):
        src, dst, dev = (
            (ppart.at[t, near], via.at[t, 0], near_dev),
            (ppart.at[t, oppo], via.at[t, 1], near_dev),
            (ppart.at[t, far], precv.at[t], far_dev),
        )[m]
        return remote(src, dst, pre_s.at[t, m], pre_r.at[t, m], dev)

    def pre_second(t):
        pre_copy(t, 1).wait_recv()
        for n in range(2):
            ppart[t, far, n] = (ppart[t, far, n].astype(F32) + via[t, 1, n].astype(F32)).astype(BF16)
        pre_copy(t, 2).start()

    def rows_copy(t, m):
        there, dev = ((p, sib_dev), (p, pair_dev), (pair, sib_dev))[m]
        part = pl.ds(2 * t, 2)
        return remote(xs.at[there, part], xs.at[there, part], xl_s.at[t, m], xl_r.at[t, m], dev)

    def rows_first(t):
        rows_copy(t, 0).start()

        @pl.when(jnp.logical_not(swapped))
        def _():
            rows_copy(t, 1).start()

    def rows_second(t):
        @pl.when(swapped)
        def _():
            sort_rows(t, rows_ref, xhome, pair)

        @pl.when(jnp.logical_not(swapped))
        def _():
            there, part = pair, pl.ds(2 * t, 2)
            remote(
                xs.at[there, part], xs.at[there, part], xl_s.at[t, 1], xl_r.at[t, 1], pair_dev
            ).wait_recv()

        rows_copy(t, 2).start()

    input_wait((1, 2, 3))
    sort_rows(0, rows, xraw, p)
    for n in range(4):
        local(n).wait()
    pre_chunk(0, p)
    forward(0)
    for n in range(4):
        own_to_sib(n).wait_recv()
    pre_chunk(0, sib)
    for n in range(1, 4):
        forward(n)
    input_start((0,))
    pre_chunk(0, pair)
    for n in range(4):
        pair_to_sib(n).wait_recv()
    pre_chunk(0, diag)
    pre_copy(0, 1).start()
    pre_copy(0, 0).start()
    home.wait()
    forward(4)
    for n in (4, 5):
        local(n).wait()
        own_to_sib(n).wait_recv()
    forward(5)
    pre_second(0)
    input_start((4,))
    rows_first(0)
    input_wait((0,))

    def hid_copy(i, m):
        src, dst, dev = (
            (hpart.at[i, near], hvia.at[i, 0], near_dev),
            (hpart.at[i, oppo], hvia.at[i, 1], near_dev),
            (hpart.at[i, far], hrecv.at[i], far_dev),
        )[m]
        return remote(src, dst, hid_s.at[i, m], hid_r.at[i, m], dev)

    def act_copy(i, m):
        q, dev = ((e, near_dev), (e, far_dev), (far, near_dev))[m]
        return remote(act.at[i, q], act.at[i, q], act_s.at[i, m], act_r.at[i, m], dev)

    def act_arrival(i, m):
        q, dev = ((near, near_dev), (far, far_dev), (oppo, near_dev))[m]
        return remote(act.at[i, q], act.at[i, q], act_s.at[i, m], act_r.at[i, m], dev)

    def pass_on(i):
        act_arrival(i, 1).wait_recv()
        act_copy(i, 2).start()

    def late_copy(i, m):
        there, dev = ((sib, sib_dev), (pair, pair_dev), (diag, diag_dev))[m]
        return remote(act.at[i, there], actlate.at[p, i], al_s.at[i, m], al_r.at[i, m], dev)

    def weight_grad(there, grads, first, layers):
        flat = xs[there, first:first + layers].reshape(layers * tokens, xs.shape[3])
        return [
            dot_tn(flat, grads[first:first + layers, n].reshape(layers * tokens, act.shape[4])) for n in range(2)
        ]

    def add_others(there, m, first, layers):
        for i in range(first, first + layers):
            late_copy(i, m).wait_recv()
        for n, grad in enumerate(weight_grad(there, actlate.at[there], first, layers)):
            keep[n] += grad

    def rows_arrive(t, m):
        there, part = ((sib, diag)[m // 2], pl.ds(2 * t, 2))
        remote(xs.at[there, part], xs.at[there, part], xl_s.at[t, m], xl_r.at[t, m], sib_dev).wait_recv()

    early = 2 * (steps - 1)

    def st_copy(t, c):
        return remote(sn.at[t, c], st.at[t + 1, c], st_s.at[t, c], st_r.at[t, c], below if c == 0 else above)

    def back_copy(c):
        return remote(sn.at[steps - 1, c], back.at[c], back_s.at[c], back_r.at[c], pair_dev)

    def step(t, carry):
        for c in range(2):
            i = 2 * t + c

            @pl.when(t > 0)
            def _():
                st_copy(t - 1, c).wait_recv()

            weight = jnp.sum(jnp.where(chosen(rows, i), comb[i], 0.0), axis=1, keepdims=True)
            slot_grads = (weight * st[t, c].astype(F32)).astype(BF16)
            if c == 0:
                @pl.when(t == 0)
                def _():
                    for n in (4, 5):
                        pair_to_sib(n).wait_recv()

            for m, q in ((1, oppo), (0, near)):
                hpart[i, q] = dot_nt(slot_grads, wda[q]).astype(BF16)
                hid_copy(i, m).start()
            for q in (far, e):
                hpart[i, q] = dot_nt(slot_grads, wda[q]).astype(BF16)

        for c in range(2):
            i = 2 * t + c
            hid_copy(i, 1).wait_recv()
            hpart[i, far] = (hpart[i, far].astype(F32) + hvia[i, 1].astype(F32)).astype(BF16)
            hid_copy(i, 2).start()

        pre_copy(t, 0).wait_recv()
        pre_copy(t, 2).wait_recv()
        pre_gate, pre_up = (
            ppart[t, e, n].astype(F32) + via[t, 0, n].astype(F32) + precv[t, n].astype(F32) for n in range(2)
        )
        sigma = jax.nn.sigmoid(pre_gate)
        ab[0] = pre_up * sigma * (1.0 + pre_gate * (1.0 - sigma))
        ab[1] = pre_gate * sigma

        for c in range(2):
            i = 2 * t + c
            for m in (0, 2):
                hid_copy(i, m).wait_recv()
            hidden = hpart[i, e].astype(F32) + hvia[i, 0].astype(F32) + hrecv[i].astype(F32)
            act[i, e, 0] = (hidden * ab[0, c * tokens:(c + 1) * tokens]).astype(BF16)
            act[i, e, 1] = (hidden * ab[1, c * tokens:(c + 1) * tokens]).astype(BF16)
            act_copy(i, 1).start()
            act_copy(i, 0).start()

        rows_second(t)
        for ahead in range(1, steps):
            @pl.when(t == ahead - 1)
            def _():
                input_wait((3 + ahead,))

        @pl.when(t < steps - 1)
        def _():
            sort_rows(t + 1, rows, xraw, p)
            pre_chunk(t + 1, oppo)
            pre_chunk(t + 1, near)
            pass_on(2 * t)
            pre_chunk(t + 1, far)
            pass_on(2 * t + 1)
            pre_copy(t + 1, 1).start()
            pre_copy(t + 1, 0).start()
            rows_first(t + 1)
            pre_chunk(t + 1, e)

        for ahead in range(2, steps):
            @pl.when(t == ahead - 2)
            def _():
                input_start((3 + ahead,))

        @pl.when(t == steps - 1)
        def _():
            for n, grad in enumerate(weight_grad(p, act.at[:, p], 0, early)):
                keep[n] = grad
            pass_on(2 * t)
            for ahead in range(steps - 1):
                rows_arrive(ahead, 0)
            add_others(sib, 0, 0, early)
            pass_on(2 * t + 1)
            add_others(pair, 1, 0, early)
            for ahead in range(steps - 1):
                rows_arrive(ahead, 2)
            add_others(diag, 2, 0, early)

        for c in range(2):
            i = 2 * t + c
            total = st[t, c].astype(F32)
            for q in (e, far, near):
                if q is near:
                    act_arrival(i, 0).wait_recv()
                total += dot_nt(act[i, q, 0], wga[q]) + dot_nt(act[i, q, 1], wua[q])
            act_arrival(i, 2).wait_recv()

            total += dot_nt(act[i, oppo, 0], wga[oppo]) + dot_nt(act[i, oppo, 1], wua[oppo])
            sn[t, c] = total.astype(BF16)

            @pl.when(t < steps - 1)
            def _():
                st_copy(t, c).start()

            for m in (2, 1, 0):
                late_copy(i, m).start()

        @pl.when(t < steps - 1)
        def _():
            pre_second(t + 1)

        return carry

    lax.fori_loop(0, steps, step, 0)

    @pl.when(swapped)
    def _():
        for c in range(2):
            back_copy(c).start()

    for n, grad in enumerate(weight_grad(p, act.at[:, p], early, 2)):
        keep[n] += grad
    rows_arrive(steps - 1, 0)
    add_others(sib, 0, early, 2)
    rows_arrive(steps - 1, 2)
    add_others(diag, 2, early, 2)
    add_others(pair, 1, early, 2)
    for n, out in ((0, gg_out), (1, gu_out)):
        out[...] = keep[n].astype(BF16)

    @pl.when(swapped)
    def _():
        for c in range(2):
            back_copy(c).wait_recv()
            state_out[c] = back[c]

    @pl.when(jnp.logical_not(swapped))
    def _():
        state_out[...] = sn[steps - 1]

    @pl.when(swapped)
    def _():
        for m in range(3 + steps):
            swap_copy(m).wait_send()
        for c in range(2):
            back_copy(c).wait_send()

    for n in range(6):
        own_to_pair(n).wait_send()
        own_to_sib(n).wait_send()
        pair_to_sib(n).wait_send()
    def drain(t, carry):
        for m in range(3):
            pre_copy(t, m).wait_send()
            for c in range(2):
                hid_copy(2 * t + c, m).wait_send()
                act_copy(2 * t + c, m).wait_send()
                late_copy(2 * t + c, m).wait_send()
        rows_copy(t, 0).wait_send()
        rows_copy(t, 2).wait_send()

        @pl.when(jnp.logical_not(swapped))
        def _():
            rows_copy(t, 1).wait_send()

        return carry

    lax.fori_loop(0, steps, drain, 0)
    for t in range(steps - 1):
        for c in range(2):
            st_copy(t, c).wait_send()


def on_device(state_in, saved_inputs, slot_rows, combine, w_gate, w_up, w_down):
    steps, _, _, tokens, width = saved_inputs.shape
    hidden = w_gate.shape[2]
    layers = 2 * steps
    sems = pltpu.SemaphoreType.DMA
    vmem = pl.BlockSpec(memory_space=pltpu.VMEM)
    anywhere = pl.BlockSpec(memory_space=pl.ANY)
    state_out, grad_gate, grad_up = pl.pallas_call(
        relay_kernel,
        out_shape=(
            jax.ShapeDtypeStruct((2, tokens, width), BF16),
            jax.ShapeDtypeStruct((width, hidden), BF16),
            jax.ShapeDtypeStruct((width, hidden), BF16),
        ),
        in_specs=[anywhere, anywhere, vmem, vmem] + [anywhere] * 3,
        out_specs=(vmem, vmem, vmem),
        scratch_shapes=[
            pltpu.VMEM((layers, tokens, width), BF16),
            pltpu.VMEM((layers, tokens, width), BF16),
            pltpu.VMEM((layers, 1, tokens), jnp.int32),
            pltpu.VMEM((layers, 1, tokens), F32),
            pltpu.VMEM((4, layers, tokens, width), BF16),
            pltpu.VMEM((4, width, hidden), BF16),
            pltpu.VMEM((4, width, hidden), BF16),
            pltpu.VMEM((4, hidden, width), BF16),
            pltpu.VMEM((steps, 2, tokens, width), BF16),
            pltpu.VMEM((steps, 2, tokens, width), BF16),
            pltpu.VMEM((2, tokens, width), BF16),
            pltpu.VMEM((steps, 4, 2, 2 * tokens, hidden), BF16),
            pltpu.VMEM((steps, 2, 2, 2 * tokens, hidden), BF16),
            pltpu.VMEM((steps, 2, 2 * tokens, hidden), BF16),
            pltpu.VMEM((2, 2 * tokens, hidden), F32),
            pltpu.VMEM((layers, 4, tokens, hidden), BF16),
            pltpu.VMEM((layers, 2, tokens, hidden), BF16),
            pltpu.VMEM((layers, tokens, hidden), BF16),
            pltpu.VMEM((layers, 4, 2, tokens, hidden), BF16),
            pltpu.VMEM((4, layers, 2, tokens, hidden), BF16),
            pltpu.VMEM((2, width, hidden), F32),
            sems((6,)), sems((1,)), sems((6,)), sems((6,)), sems((6,)), sems((6,)), sems((6,)), sems((6,)),
            sems((3 + steps,)), sems((3 + steps,)),
            sems((steps, 3)), sems((steps, 3)),
            sems((layers, 3)), sems((layers, 3)),
            sems((layers, 3)), sems((layers, 3)),
            sems((steps - 1, 2)), sems((steps - 1, 2)),
            sems((2,)), sems((2,)),
            sems((steps, 3)), sems((steps, 3)),
            sems((layers, 3)), sems((layers, 3)),
        ],
        compiler_params=pltpu.CompilerParams(
            collective_id=0, has_side_effects=True, vmem_limit_bytes=56 * 2**20
        ),
        cost_estimate=pl.CostEstimate(
            flops=2 * layers * tokens * width * 4 * hidden * 7,
            bytes_accessed=2 * (layers * tokens * width + 5 * width * hidden),
            transcendentals=layers * tokens * hidden,
        ),
        name="relay",
    )(
        state_in[:, 0],
        saved_inputs.reshape(layers, tokens, width),
        slot_rows.reshape(layers, 1, tokens),
        combine.reshape(layers, 1, tokens),
        w_gate[0],
        w_up[0],
        w_down[0],
    )
    return state_out[:, None], grad_gate[None], grad_up[None]


def solution(mesh):
    placed = (
        P(None, "section", "dp", "expert"),
        P(None, None, "section", "dp", "expert"),
        P(None, None, "section", "dp"),
        P(None, None, "section", "dp"),
        P("section", "expert", "dp"),
        P("section", "expert", "dp"),
        P("section", "dp", "expert"),
    )
    return jax.shard_map(
        on_device,
        mesh=mesh,
        in_specs=placed,
        out_specs=(
            P(None, "section", "dp", "expert"),
            P("section", "expert", "dp"),
            P("section", "expert", "dp"),
        ),
        check_vma=False,
    )
```

```python
import jax
import jax.numpy as jnp
from jax import lax
from jax.experimental import pallas as pl
from jax.experimental.pallas import tpu as pltpu
from jax.sharding import PartitionSpec as P

MESH = pl.DeviceIdType.MESH
F32 = jnp.float32
BF16 = jnp.bfloat16


def dot_nn(a, b):
    return lax.dot_general(a, b, (((1,), (0,)), ((), ())), preferred_element_type=F32)


def dot_nt(a, b):
    return lax.dot_general(a, b, (((1,), (1,)), ((), ())), preferred_element_type=F32)


def dot_tn(a, b):
    return lax.dot_general(a, b, (((0,), (0,)), ((), ())), preferred_element_type=F32)


def relay_kernel(
    state_ref, x_ref, rows_ref, comb_ref, wg_ref, wu_ref, wd_ref,
    state_out, gg_out, gu_out,
    xraw, xhome, rows, comb, xs, wga, wua, wda, st, sn, back, ppart, via, precv, ab, hpart, hvia, hrecv, act,
    actlate, keep,
    loc_sem, home_sem, ws_send, ws_recv, wp_send, wp_recv, wf_send, wf_recv, in_s, in_r,
    pre_s, pre_r, hid_s, hid_r, act_s, act_r, st_s, st_r, back_s, back_r, xl_s, xl_r, al_s, al_r,
):
    s = lax.axis_index("section")
    e = lax.axis_index("expert")
    p = lax.axis_index("dp")
    sections = lax.axis_size("section")
    steps = st.shape[0]
    tokens = st.shape[2]
    core = lax.rem(p, 2)
    low = lax.div(p, 2)
    sib = p + 1 - 2 * core
    pair = lax.rem(p + 2, 4)
    diag = lax.rem(sib + 2, 4)
    sib_dev = (s, e, sib)
    pair_dev = (s, e, pair)
    diag_dev = (s, e, diag)
    below = (lax.rem(s + sections - 1, sections), e, p)
    above = (lax.rem(s + 1, sections), e, p)

    swapped = lax.rem(e + core, 2) == 1
    near = lax.rem(e + 3 + 2 * low, 4)
    far = lax.rem(e + 1 + 2 * low, 4)
    oppo = lax.rem(e + 2, 4)
    near_dev = (s, near, pair)
    far_dev = (s, far, pair)
    oppo_dev = (s, oppo, p)

    def remote(src, dst, send, recv, dev):
        return pltpu.make_async_remote_copy(
            src_ref=src, dst_ref=dst, send_sem=send, recv_sem=recv,
            device_id=dev, device_id_type=MESH,
        )

    barrier = pltpu.get_barrier_semaphore()
    for dev in (near_dev, far_dev, oppo_dev, sib_dev, pair_dev, diag_dev, below, above):
        pl.semaphore_signal(barrier, inc=1, device_id=dev, device_id_type=MESH)
    pl.semaphore_wait(barrier, 8)

    def input_refs(m):
        if m == 0:
            return state_ref, st.at[0]
        if m == 1:
            return rows_ref, rows
        if m == 2:
            return comb_ref, comb
        return x_ref.at[pl.ds(2 * (m - 3), 2)], xraw.at[pl.ds(2 * (m - 3), 2)]

    def swap_copy(m):
        src, dst = input_refs(m)
        return remote(src, dst, in_s.at[m], in_r.at[m], pair_dev)

    def stay_copy(m):
        src, dst = input_refs(m)
        return pltpu.make_async_copy(src, dst, in_r.at[m])

    def input_start(members):
        @pl.when(swapped)
        def _():
            for m in members:
                swap_copy(m).start()

        @pl.when(jnp.logical_not(swapped))
        def _():
            for m in members:
                stay_copy(m).start()

    def input_wait(members):
        @pl.when(swapped)
        def _():
            for m in members:
                swap_copy(m).wait_recv()

        @pl.when(jnp.logical_not(swapped))
        def _():
            for m in members:
                stay_copy(m).wait()

    def weight_refs(n):
        src, dst = ((wg_ref, wga), (wu_ref, wua), (wd_ref, wda))[n // 2]
        depth = src.shape[0] // 2
        return src, dst, pl.ds((n % 2) * depth, depth)

    def own_to_pair(n):
        src, dst, part = weight_refs(n)
        return remote(src.at[part], dst.at[p, part], wp_send.at[n], wp_recv.at[n], pair_dev)

    def own_to_sib(n):
        src, dst, part = weight_refs(n)
        return remote(src.at[part], dst.at[p, part], ws_send.at[n], ws_recv.at[n], sib_dev)

    def pair_to_sib(n):
        src, dst, part = weight_refs(n)
        return remote(dst.at[pair, part], dst.at[pair, part], wf_send.at[n], wf_recv.at[n], sib_dev)

    def local(n):
        src, dst, part = weight_refs(n)
        return pltpu.make_async_copy(src.at[part], dst.at[p, part], loc_sem.at[n])

    def forward(n):
        own_to_pair(n).wait_recv()
        pair_to_sib(n).start()
        if n + 3 < 6:
            own_to_pair(n + 3).start()

    home = pltpu.make_async_copy(x_ref, xhome, home_sem.at[0])

    input_start((1, 2, 3))
    for n in range(3):
        own_to_pair(n).start()
    for n in range(6):
        local(n).start()
        own_to_sib(n).start()
    home.start()

    def chosen(of, i):
        token = lax.broadcasted_iota(jnp.int32, (tokens, tokens), 0)
        return token == of[i]

    def sort_rows(t, of, raw, there):
        for c in range(2):
            i = 2 * t + c
            pick = jnp.where(chosen(of, i), 1.0, 0.0).astype(BF16)
            xs[there, i] = dot_nn(pick, raw[i]).astype(BF16)

    def pre_chunk(t, q):
        x = xs[p, pl.ds(2 * t, 2)].reshape(2 * tokens, xs.shape[3])
        ppart[t, q, 0] = dot_nn(x, wga[q]).astype(BF16)
        ppart[t, q, 1] = dot_nn(x, wua[q]).astype(BF16)

    def pre_copy(t, m):
        src, dst, dev = (
            (ppart.at[t, near], via.at[t, 0], near_dev),
            (ppart.at[t, oppo], via.at[t, 1], near_dev),
            (ppart.at[t, far], precv.at[t], far_dev),
        )[m]
        return remote(src, dst, pre_s.at[t, m], pre_r.at[t, m], dev)

    def pre_second(t):
        pre_copy(t, 1).wait_recv()
        for n in range(2):
            ppart[t, far, n] = (ppart[t, far, n].astype(F32) + via[t, 1, n].astype(F32)).astype(BF16)
        pre_copy(t, 2).start()

    def rows_copy(t, m):
        there, dev = ((p, sib_dev), (p, pair_dev), (pair, sib_dev))[m]
        part = pl.ds(2 * t, 2)
        return remote(xs.at[there, part], xs.at[there, part], xl_s.at[t, m], xl_r.at[t, m], dev)

    def rows_first(t):
        rows_copy(t, 0).start()

        @pl.when(jnp.logical_not(swapped))
        def _():
            rows_copy(t, 1).start()

    def rows_second(t):
        @pl.when(swapped)
        def _():
            sort_rows(t, rows_ref, xhome, pair)

        @pl.when(jnp.logical_not(swapped))
        def _():
            there, part = pair, pl.ds(2 * t, 2)
            remote(
                xs.at[there, part], xs.at[there, part], xl_s.at[t, 1], xl_r.at[t, 1], pair_dev
            ).wait_recv()

        rows_copy(t, 2).start()

    input_wait((1, 2, 3))
    sort_rows(0, rows, xraw, p)
    for n in range(4):
        local(n).wait()
    pre_chunk(0, p)
    forward(0)
    for n in range(4):
        own_to_sib(n).wait_recv()
    pre_chunk(0, sib)
    for n in range(1, 4):
        forward(n)
    input_start((0,))
    pre_chunk(0, pair)
    for n in range(4):
        pair_to_sib(n).wait_recv()
    pre_chunk(0, diag)
    pre_copy(0, 1).start()
    pre_copy(0, 0).start()
    home.wait()
    forward(4)
    for n in (4, 5):
        local(n).wait()
        own_to_sib(n).wait_recv()
    forward(5)
    pre_second(0)
    input_start((4,))
    rows_first(0)
    input_wait((0,))

    def hid_copy(i, m):
        src, dst, dev = (
            (hpart.at[i, near], hvia.at[i, 0], near_dev),
            (hpart.at[i, oppo], hvia.at[i, 1], near_dev),
            (hpart.at[i, far], hrecv.at[i], far_dev),
        )[m]
        return remote(src, dst, hid_s.at[i, m], hid_r.at[i, m], dev)

    def act_copy(i, m):
        q, dev = ((e, near_dev), (e, far_dev), (far, near_dev))[m]
        return remote(act.at[i, q], act.at[i, q], act_s.at[i, m], act_r.at[i, m], dev)

    def act_arrival(i, m):
        q, dev = ((near, near_dev), (far, far_dev), (oppo, near_dev))[m]
        return remote(act.at[i, q], act.at[i, q], act_s.at[i, m], act_r.at[i, m], dev)

    def pass_on(i):
        act_arrival(i, 1).wait_recv()
        act_copy(i, 2).start()

    def late_copy(i, m):
        there, dev = ((sib, sib_dev), (pair, pair_dev), (diag, diag_dev))[m]
        return remote(act.at[i, there], actlate.at[p, i], al_s.at[i, m], al_r.at[i, m], dev)

    def weight_grad(there, grads, first, layers):
        flat = xs[there, first:first + layers].reshape(layers * tokens, xs.shape[3])
        return [
            dot_tn(flat, grads[first:first + layers, n].reshape(layers * tokens, act.shape[4])) for n in range(2)
        ]

    def add_others(there, m, first, layers):
        for i in range(first, first + layers):
            late_copy(i, m).wait_recv()
        for n, grad in enumerate(weight_grad(there, actlate.at[there], first, layers)):
            keep[n] += grad

    def rows_arrive(t, m):
        there, part = ((sib, diag)[m // 2], pl.ds(2 * t, 2))
        remote(xs.at[there, part], xs.at[there, part], xl_s.at[t, m], xl_r.at[t, m], sib_dev).wait_recv()

    early = 2 * (steps - 1)

    def st_copy(t, c):
        return remote(sn.at[t, c], st.at[t + 1, c], st_s.at[t, c], st_r.at[t, c], below if c == 0 else above)

    def back_copy(c):
        return remote(sn.at[steps - 1, c], back.at[c], back_s.at[c], back_r.at[c], pair_dev)

    def step(t, carry):
        for c in range(2):
            i = 2 * t + c

            @pl.when(t > 0)
            def _():
                st_copy(t - 1, c).wait_recv()

            weight = jnp.sum(jnp.where(chosen(rows, i), comb[i], 0.0), axis=1, keepdims=True)
            slot_grads = (weight * st[t, c].astype(F32)).astype(BF16)
            if c == 0:
                @pl.when(t == 0)
                def _():
                    for n in (4, 5):
                        pair_to_sib(n).wait_recv()

            for m, q in ((1, oppo), (0, near)):
                hpart[i, q] = dot_nt(slot_grads, wda[q]).astype(BF16)
                hid_copy(i, m).start()
            for q in (far, e):
                hpart[i, q] = dot_nt(slot_grads, wda[q]).astype(BF16)

        for c in range(2):
            i = 2 * t + c
            hid_copy(i, 1).wait_recv()
            hpart[i, far] = (hpart[i, far].astype(F32) + hvia[i, 1].astype(F32)).astype(BF16)
            hid_copy(i, 2).start()

        pre_copy(t, 0).wait_recv()
        pre_copy(t, 2).wait_recv()
        pre_gate, pre_up = (
            ppart[t, e, n].astype(F32) + via[t, 0, n].astype(F32) + precv[t, n].astype(F32) for n in range(2)
        )
        sigma = jax.nn.sigmoid(pre_gate)
        ab[0] = pre_up * sigma * (1.0 + pre_gate * (1.0 - sigma))
        ab[1] = pre_gate * sigma

        for c in range(2):
            i = 2 * t + c
            for m in (0, 2):
                hid_copy(i, m).wait_recv()
            hidden = hpart[i, e].astype(F32) + hvia[i, 0].astype(F32) + hrecv[i].astype(F32)
            act[i, e, 0] = (hidden * ab[0, c * tokens:(c + 1) * tokens]).astype(BF16)
            act[i, e, 1] = (hidden * ab[1, c * tokens:(c + 1) * tokens]).astype(BF16)
            act_copy(i, 1).start()
            act_copy(i, 0).start()

        rows_second(t)
        for ahead in range(1, steps):
            @pl.when(t == ahead - 1)
            def _():
                input_wait((3 + ahead,))

        @pl.when(t < steps - 1)
        def _():
            sort_rows(t + 1, rows, xraw, p)
            pre_chunk(t + 1, oppo)
            pre_chunk(t + 1, near)
            pass_on(2 * t)
            pre_chunk(t + 1, far)
            pass_on(2 * t + 1)
            pre_copy(t + 1, 1).start()
            pre_copy(t + 1, 0).start()
            rows_first(t + 1)
            pre_chunk(t + 1, e)

        for ahead in range(2, steps):
            @pl.when(t == ahead - 2)
            def _():
                input_start((3 + ahead,))

        @pl.when(t == steps - 1)
        def _():
            for n, grad in enumerate(weight_grad(p, act.at[:, p], 0, early)):
                keep[n] = grad
            pass_on(2 * t)
            for ahead in range(steps - 1):
                rows_arrive(ahead, 0)
            add_others(sib, 0, 0, early)
            pass_on(2 * t + 1)
            add_others(pair, 1, 0, early)
            for ahead in range(steps - 1):
                rows_arrive(ahead, 2)
            add_others(diag, 2, 0, early)

        for c in range(2):
            i = 2 * t + c
            total = st[t, c].astype(F32)
            for q in (e, far, near):
                if q is near:
                    act_arrival(i, 0).wait_recv()
                total += dot_nt(act[i, q, 0], wga[q]) + dot_nt(act[i, q, 1], wua[q])
            act_arrival(i, 2).wait_recv()

            total += dot_nt(act[i, oppo, 0], wga[oppo]) + dot_nt(act[i, oppo, 1], wua[oppo])
            sn[t, c] = total.astype(BF16)

            @pl.when(t < steps - 1)
            def _():
                st_copy(t, c).start()

            if c == 0:
                for m in (2, 1, 0):
                    late_copy(i, m).start()

        @pl.when(t < steps - 1)
        def _():
            pre_second(t + 1)

        for m in (2, 1, 0):
            late_copy(2 * t + 1, m).start()

        return carry

    lax.fori_loop(0, steps, step, 0)

    @pl.when(swapped)
    def _():
        for c in range(2):
            back_copy(c).start()

    for n, grad in enumerate(weight_grad(p, act.at[:, p], early, 2)):
        keep[n] += grad
    rows_arrive(steps - 1, 0)
    add_others(sib, 0, early, 2)
    rows_arrive(steps - 1, 2)
    add_others(diag, 2, early, 2)
    add_others(pair, 1, early, 2)
    for n, out in ((0, gg_out), (1, gu_out)):
        out[...] = keep[n].astype(BF16)

    @pl.when(swapped)
    def _():
        for c in range(2):
            back_copy(c).wait_recv()
            state_out[c] = back[c]

    @pl.when(jnp.logical_not(swapped))
    def _():
        state_out[...] = sn[steps - 1]

    @pl.when(swapped)
    def _():
        for m in range(3 + steps):
            swap_copy(m).wait_send()
        for c in range(2):
            back_copy(c).wait_send()

    for n in range(6):
        own_to_pair(n).wait_send()
        own_to_sib(n).wait_send()
        pair_to_sib(n).wait_send()
    def drain(t, carry):
        for m in range(3):
            pre_copy(t, m).wait_send()
            for c in range(2):
                hid_copy(2 * t + c, m).wait_send()
                act_copy(2 * t + c, m).wait_send()
                late_copy(2 * t + c, m).wait_send()
        rows_copy(t, 0).wait_send()
        rows_copy(t, 2).wait_send()

        @pl.when(jnp.logical_not(swapped))
        def _():
            rows_copy(t, 1).wait_send()

        return carry

    lax.fori_loop(0, steps, drain, 0)
    for t in range(steps - 1):
        for c in range(2):
            st_copy(t, c).wait_send()


def on_device(state_in, saved_inputs, slot_rows, combine, w_gate, w_up, w_down):
    steps, _, _, tokens, width = saved_inputs.shape
    hidden = w_gate.shape[2]
    layers = 2 * steps
    sems = pltpu.SemaphoreType.DMA
    vmem = pl.BlockSpec(memory_space=pltpu.VMEM)
    anywhere = pl.BlockSpec(memory_space=pl.ANY)
    state_out, grad_gate, grad_up = pl.pallas_call(
        relay_kernel,
        out_shape=(
            jax.ShapeDtypeStruct((2, tokens, width), BF16),
            jax.ShapeDtypeStruct((width, hidden), BF16),
            jax.ShapeDtypeStruct((width, hidden), BF16),
        ),
        in_specs=[anywhere, anywhere, vmem, vmem] + [anywhere] * 3,
        out_specs=(vmem, vmem, vmem),
        scratch_shapes=[
            pltpu.VMEM((layers, tokens, width), BF16),
            pltpu.VMEM((layers, tokens, width), BF16),
            pltpu.VMEM((layers, 1, tokens), jnp.int32),
            pltpu.VMEM((layers, 1, tokens), F32),
            pltpu.VMEM((4, layers, tokens, width), BF16),
            pltpu.VMEM((4, width, hidden), BF16),
            pltpu.VMEM((4, width, hidden), BF16),
            pltpu.VMEM((4, hidden, width), BF16),
            pltpu.VMEM((steps, 2, tokens, width), BF16),
            pltpu.VMEM((steps, 2, tokens, width), BF16),
            pltpu.VMEM((2, tokens, width), BF16),
            pltpu.VMEM((steps, 4, 2, 2 * tokens, hidden), BF16),
            pltpu.VMEM((steps, 2, 2, 2 * tokens, hidden), BF16),
            pltpu.VMEM((steps, 2, 2 * tokens, hidden), BF16),
            pltpu.VMEM((2, 2 * tokens, hidden), F32),
            pltpu.VMEM((layers, 4, tokens, hidden), BF16),
            pltpu.VMEM((layers, 2, tokens, hidden), BF16),
            pltpu.VMEM((layers, tokens, hidden), BF16),
            pltpu.VMEM((layers, 4, 2, tokens, hidden), BF16),
            pltpu.VMEM((4, layers, 2, tokens, hidden), BF16),
            pltpu.VMEM((2, width, hidden), F32),
            sems((6,)), sems((1,)), sems((6,)), sems((6,)), sems((6,)), sems((6,)), sems((6,)), sems((6,)),
            sems((3 + steps,)), sems((3 + steps,)),
            sems((steps, 3)), sems((steps, 3)),
            sems((layers, 3)), sems((layers, 3)),
            sems((layers, 3)), sems((layers, 3)),
            sems((steps - 1, 2)), sems((steps - 1, 2)),
            sems((2,)), sems((2,)),
            sems((steps, 3)), sems((steps, 3)),
            sems((layers, 3)), sems((layers, 3)),
        ],
        compiler_params=pltpu.CompilerParams(
            collective_id=0, has_side_effects=True, vmem_limit_bytes=56 * 2**20
        ),
        cost_estimate=pl.CostEstimate(
            flops=2 * layers * tokens * width * 4 * hidden * 7,
            bytes_accessed=2 * (layers * tokens * width + 5 * width * hidden),
            transcendentals=layers * tokens * hidden,
        ),
        name="relay",
    )(
        state_in[:, 0],
        saved_inputs.reshape(layers, tokens, width),
        slot_rows.reshape(layers, 1, tokens),
        combine.reshape(layers, 1, tokens),
        w_gate[0],
        w_up[0],
        w_down[0],
    )
    return state_out[:, None], grad_gate[None], grad_up[None]


def solution(mesh):
    placed = (
        P(None, "section", "dp", "expert"),
        P(None, None, "section", "dp", "expert"),
        P(None, None, "section", "dp"),
        P(None, None, "section", "dp"),
        P("section", "expert", "dp"),
        P("section", "expert", "dp"),
        P("section", "dp", "expert"),
    )
    return jax.shard_map(
        on_device,
        mesh=mesh,
        in_specs=placed,
        out_specs=(
            P(None, "section", "dp", "expert"),
            P("section", "expert", "dp"),
            P("section", "expert", "dp"),
        ),
        check_vma=False,
    )
```
